32 devices in a mesh: row: 4 (over y, core), col: 8 (over z, x).
Axes of the slice: x: 2, y: 2, z: 4, core: 2. Of those that a mesh axis runs over, the one named last changes fastest.
Arguments:
- vectors: float32 [16, 49152], P(None, ('row', 'col')), may hold values from -6 to 6
- tiles: float32 [4, 8, 48, 256, 256], P('row', 'col'), may hold values from -0.375 to 0.375
- tile_rows: int32 [4, 8, 48], P('row', 'col'), may hold values from 0 to 47, as said below
- tile_cols: int32 [4, 8, 48], P('row', 'col'), may hold values from 0 to 23, as said below
- counts: int32 [4, 8], P('row', 'col'), may hold values from 6 to 48, as said below
Outputs:
- residual: float32 [16, 49152], P(None, ('row', 'col'))
- image: float32 [16, 49152], P(None, ('row', 'col'))
- gram: float32 [16, 16], replicated
The draws below stay inside these ranges and needn't reach their ends.
Inputs may be any that keep to these rules, and one draw needn't show every extreme that they name: Within one cell the slots name distinct tile positions. The live slots of one cell name at most 3 distinct block rows within any one segment (tile_rows // 6 equal), and every cell has a segment with exactly 3. The live slots of one cell name at most 3 distinct block columns within any one segment (tile_cols // 6 equal), and every cell has a segment with exactly 3. `counts`: some cell holds all 48 slots live in every draw; slots at or above a cell's count hold unused tiles.
All inputs are finite; a program needn't handle non-finite values.
Results may differ from the reference program's by a relative error of at most 0.0001.
Values sent between devices are 32-bit elements; how exact they have to be, the bound alone decides.
A program may use at most 64 MiB of HBM per device.

```python
import jax
import jax.numpy as jnp
from jax import lax

NV = 16
TILE = 256
SEGB = 6
MAXT = 48
CAP = 3
ORDER = 49152
N_ROW = 4
N_COL = 8


def draw_positions(key):
    row_space = N_COL * CAP
    col_space = N_ROW * CAP
    total = row_space * col_space
    keys = jax.random.split(key, N_ROW * N_COL)
    cell_ids = jnp.arange(N_ROW * N_COL, dtype=jnp.int32)
    forced_index = jnp.arange(CAP, dtype=jnp.int32)
    forced = ((N_COL - 1) * CAP + forced_index) * col_space + (N_ROW - 1) * CAP + forced_index

    def one_cell(single, cell):
        first, second, third = jax.random.split(single, 3)
        scores = jax.random.permutation(first, total).astype(jnp.int32)
        scores = scores.at[forced].set(-1 - forced_index)
        picked = jnp.argsort(scores, stable=True)[:MAXT].astype(jnp.int32)
        row_comp = picked // col_space
        col_comp = picked % col_space
        row_shift = jax.random.randint(second, (), 0, SEGB)
        col_shift = jax.random.randint(third, (), 0, SEGB)
        row_shift = jnp.where(cell == 0, SEGB - CAP, row_shift)
        col_shift = jnp.where(cell == 0, SEGB - CAP, col_shift)
        rows = row_comp // CAP * SEGB + (row_comp % CAP + row_shift) % SEGB
        cols = col_comp // CAP * SEGB + (col_comp % CAP + col_shift) % SEGB
        return (rows.astype(jnp.int32), cols.astype(jnp.int32))
    rows, cols = jax.vmap(one_cell)(keys, cell_ids)
    return (rows.reshape(N_ROW, N_COL, MAXT), cols.reshape(N_ROW, N_COL, MAXT))


def draw_tile_rows(key, part):
    rows, cols = draw_positions(key)
    return rows.astype(jnp.int32)


def draw_tile_cols(key, part):
    rows, cols = draw_positions(key)
    return cols.astype(jnp.int32)


def draw_counts(key, part):
    key = jax.random.fold_in(key, 7)
    first, second, third = jax.random.split(key, 3)
    base = jax.random.randint(first, (N_ROW, N_COL), MAXT // 8, MAXT // 3 + 1)
    heavy = jax.random.randint(second, (N_ROW, N_COL), 0, 16) == 0
    base = jnp.where(heavy, MAXT, base)
    where_full = jax.random.randint(third, (), 0, N_ROW * N_COL)
    flat = base.reshape(-1).at[where_full].set(MAXT)
    return flat.reshape(N_ROW, N_COL).astype(jnp.int32)


def shard_levels(key, dims, shards, smallest, largest):
    def one(dim, shards_of):
        heights = jax.random.uniform(jax.random.fold_in(jax.random.fold_in(key, 6), dim), (shards_of,), jnp.float32, smallest / len(shards), largest / len(shards))
        return jnp.repeat(jnp.exp(heights), dims[dim] // shards_of).reshape((-1,) + (1,) * (len(dims) - dim - 1))

    factor_of = one(*shards[0])
    for cut in shards[1:]:
        factor_of = factor_of * one(*cut)
    return factor_of


def normal_values(rng, extent, scale, limit, shards=(), kind=jnp.bfloat16):
    values = scale * jax.random.normal(rng, extent, jnp.float32)
    if shards:
        values = values * shard_levels(rng, extent, shards, -0.22, 0.18)
    return jnp.clip(values, -limit, limit).astype(kind)


def setup_inputs(seed: int = 0) -> dict:
    seeds = jax.random.split(jax.random.key(seed), 6)
    return {
        "vectors": normal_values(seeds[0], (NV, ORDER), 1.0, 6.0, ((1, 32),), jnp.float32),
        "tiles": normal_values(seeds[1], (N_ROW, N_COL, MAXT, TILE, TILE), TILE ** -0.5, 0.375, ((0, 4), (1, 8)), jnp.float32),
        "tile_rows": draw_tile_rows(jax.random.fold_in(seeds[5], 71), 0),
        "tile_cols": draw_tile_cols(jax.random.fold_in(seeds[5], 71), 0),
        "counts": draw_counts(jax.random.fold_in(seeds[5], 71), 0),
    }


def block_indices(tile_rows, tile_cols):
    row_ids = jnp.arange(N_ROW, dtype=jnp.int32)[:, None, None]
    col_ids = jnp.arange(N_COL, dtype=jnp.int32)[None, :, None]
    global_rows = row_ids * (N_COL * SEGB) + tile_rows
    global_cols = (tile_cols // SEGB * N_COL + col_ids) * SEGB + tile_cols % SEGB
    return (global_rows.astype(jnp.int32), global_cols.astype(jnp.int32))

def apply_hamiltonian(block, tiles, global_rows, global_cols, live):
    blocks = block.reshape(NV, ORDER // TILE, TILE)
    flat_tiles = tiles.reshape(N_ROW * N_COL, MAXT, TILE, TILE)
    flat_rows = global_rows.reshape(N_ROW * N_COL, MAXT)
    flat_cols = global_cols.reshape(N_ROW * N_COL, MAXT)
    flat_live = live.reshape(N_ROW * N_COL, MAXT)

    def step(total, items):
        cell_tiles, rows, cols, alive = items
        masked = cell_tiles * alive[:, None, None]
        from_cols = blocks[:, cols, :]
        from_rows = blocks[:, rows, :]
        to_rows = jnp.einsum('kij,vkj->vki', masked, from_cols, precision=lax.Precision.HIGHEST)
        to_cols = jnp.einsum('kij,vki->vkj', masked, from_rows, precision=lax.Precision.HIGHEST)
        total = total.at[:, rows, :].add(to_rows)
        total = total.at[:, cols, :].add(to_cols)
        return (total, None)
    start = jnp.zeros((NV, ORDER // TILE, TILE), jnp.float32)
    total, unused = lax.scan(step, start, (flat_tiles, flat_rows, flat_cols, flat_live))
    return total.reshape(NV, ORDER)

def reference(vectors, tiles, tile_rows, tile_cols, counts):
    global_rows, global_cols = block_indices(tile_rows, tile_cols)
    slots = jnp.arange(MAXT, dtype=jnp.int32)[None, None, :]
    live = (slots < counts[:, :, None]).astype(jnp.float32)
    product = apply_hamiltonian(vectors, tiles, global_rows, global_cols, live)
    correlation = jnp.einsum('vn,wn->vw', vectors, vectors, precision=lax.Precision.HIGHEST)
    projection = jnp.einsum('vn,wn->vw', vectors, product, precision=lax.Precision.HIGHEST)
    factor = jnp.linalg.cholesky(correlation)
    coeffs = jax.scipy.linalg.cho_solve((factor, True), projection)
    residual = product - jnp.einsum('wv,wn->vn', coeffs, vectors, precision=lax.Precision.HIGHEST)
    image = apply_hamiltonian(residual, tiles, global_rows, global_cols, live)
    gram = jnp.einsum('vn,wn->vw', residual, image, precision=lax.Precision.HIGHEST) / ORDER
    return (residual, image, gram)
```

```python
import functools

import jax
import jax.numpy as jnp
from jax import lax
from jax.experimental import pallas as pl
from jax.experimental.pallas import tpu as pltpu
from jax.sharding import PartitionSpec as P

TILE = 256
CAP = 3
POS = 8
MESH = pl.DeviceIdType.MESH
F32 = jnp.float32
BF16 = jnp.bfloat16
EXACT = lax.Precision.HIGHEST


def dot_nt(a, b, precision=None):
    return lax.dot_general(
        a, b, (((1,), (1,)), ((), ())), precision=precision, preferred_element_type=F32
    )


def dot_nn(a, b, precision=None):
    return lax.dot_general(
        a, b, (((1,), (0,)), ((), ())), precision=precision, preferred_element_type=F32
    )


def split(x):
    high = x.astype(BF16)
    return high, (x - high.astype(F32)).astype(BF16)


def prep_kernel(n_row, n_col, segb, rows, cols, count, out):
    slots = rows.shape[2]
    live_count = count[0, 0]

    def clear(i, carry):
        for lane in range(POS + segb):
            out[i, 0, lane] = 0
        return carry

    lax.fori_loop(0, n_row + n_col, clear, 0)

    def touch(k, carry):
        live = (k < live_count).astype(jnp.int32)
        for ids, base in ((rows, 0), (cols, n_col)):
            which = ids[0, 0, k]
            seg = base + which // segb
            lane = POS + which % segb
            out[seg, 0, lane] = jnp.maximum(out[seg, 0, lane], live)
        return carry

    lax.fori_loop(0, slots, touch, 0)

    def rank(i, carry):
        n = 0
        for b in range(segb):
            named = out[i, 0, POS + b] > 0
            out[i, 0, POS + b] = jnp.where(named, n, CAP)
            out[i, 0, jnp.where(named, n, POS - 1)] = b
            n = n + named.astype(jnp.int32)
        return carry

    lax.fori_loop(0, n_row + n_col, rank, 0)

    def place(k, carry):
        for line, ids, base in ((n_row + n_col, rows, 0), (n_row + n_col + 1, cols, n_col)):
            which = ids[0, 0, k]
            seg = which // segb
            at = seg * CAP + out[base + seg, 0, POS + which % segb]
            out[line, 0, k] = jnp.where(k < live_count, at, -1)
        return carry

    lax.fori_loop(0, slots, place, 0)


def main_kernel(n_row, n_col, segb, order, *refs):
    (tab_s, tab_v, vec, tiles, residual, image, gram) = refs[:7]
    (
        raw, tile_hi, tile_lo, pick_r, pick_c, z_hi, z_lo, idx_v, idx_s, own,
        zr, zc, corr_1, corr_2, gram_1, gram_2, tile_sem, idx_sem,
    ) = refs[7:25]
    rounds = [refs[25:38], refs[38:51]]
    (ir_s, ir_r, ic_s, ic_r, c1_s, c1_r, c2_s, c2_r, g1_s, g1_r, g2_s, g2_r) = refs[51:63]
    nv = vec.shape[0]
    slots = raw.shape[0]
    row = lax.axis_index("row")
    col = lax.axis_index("col")
    axes = {
        "row": (n_row, row, lambda p: (p, col)),
        "col": (n_col, col, lambda p: (row, p)),
    }

    def each_peer(axis, body):
        n, me, device = axes[axis]

        def step(d, carry):
            body(lax.rem(me + d, n))
            return carry

        lax.fori_loop(1, n, step, 0)

    def copy(axis, source, target, send, recv, p, slot):
        return pltpu.make_async_remote_copy(
            src_ref=source, dst_ref=target, send_sem=send.at[p], recv_sem=recv.at[slot],
            device_id=axes[axis][2](p), device_id_type=MESH,
        )

    class Exchange:
        def __init__(self, axis, source, target, send, recv):
            self.axis, self.source, self.target = axis, source, target
            self.send, self.recv = send, recv

        def make(self, p, slot):
            return copy(self.axis, self.source(p), self.target(slot), self.send, self.recv, p, slot)

        def start(self):
            me = axes[self.axis][1]
            each_peer(self.axis, lambda p: self.make(p, me).start())

        def wait_recv(self):
            each_peer(self.axis, lambda p: self.make(p, p).wait_recv())

        def wait_send(self):
            me = axes[self.axis][1]
            each_peer(self.axis, lambda p: self.make(p, me).wait_send())

    chunk = 8 if slots % 8 == 0 else 1
    n_chunks = slots // chunk
    tile_copies = [
        pltpu.make_async_copy(
            tiles.at[0, 0, pl.ds(i * chunk, chunk)], raw.at[pl.ds(i * chunk, chunk)], tile_sem.at[i]
        )
        for i in range(n_chunks)
    ]
    for c in tile_copies:
        c.start()

    barrier = pltpu.get_barrier_semaphore()
    for axis in ("row", "col"):
        device = axes[axis][2]
        each_peer(
            axis,
            lambda p: pl.semaphore_signal(
                barrier, inc=1, device_id=device(p), device_id_type=MESH
            ),
        )
    idx_v[col] = tab_v[col]
    idx_v[n_col + row] = tab_v[n_col + row]
    corr_1[...] = jnp.zeros_like(corr_1)
    corr_2[...] = jnp.zeros_like(corr_2)
    gram_1[...] = jnp.zeros_like(gram_1)
    gram_2[...] = jnp.zeros_like(gram_2)
    zero_block = jnp.zeros((nv, TILE), F32)
    for r in rounds:
        back_r, back_c = r[4], r[5]
        for i in range(n_col):
            back_r[i, CAP] = zero_block
        for i in range(n_row):
            back_c[i, CAP] = zero_block
    pl.semaphore_wait(barrier, n_row + n_col - 2)

    idx_r = Exchange("col", lambda p: tab_v.at[p], lambda i: idx_v.at[i], ir_s, ir_r)
    idx_c = Exchange("row", lambda p: tab_v.at[n_col + p], lambda i: idx_v.at[n_col + i], ic_s, ic_r)
    idx_r.start()
    idx_c.start()
    for b in range(segb):
        own[0, b] = vec[:, b * TILE:(b + 1) * TILE]
    idx_c.wait_recv()
    idx_r.wait_recv()
    to_smem = pltpu.make_async_copy(idx_v, idx_s, idx_sem)
    to_smem.start()
    to_smem.wait()

    def build_pick(line, pick):
        n, wide = pick.shape
        lane = lax.broadcasted_iota(jnp.int32, (8, wide), 1)
        slot_of, vector_of = lane // nv, lane % nv

        def step(k, carry):
            return jnp.where(slot_of == k, vector_of + nv * tab_s[line, 0, k], carry)

        wanted = lax.fori_loop(0, slots, step, jnp.full((8, wide), -1, jnp.int32))[0:1]
        part = CAP * nv

        def fill(i, carry):
            at = lax.broadcasted_iota(jnp.int32, (part, wide), 0) + i * part
            pick[pl.ds(pl.multiple_of(i * part, part), part), :] = jnp.where(
                at == wanted, 1.0, 0.0
            ).astype(BF16)
            return carry

        lax.fori_loop(0, n // part, fill, 0)

    def split_tiles():
        for i in range(n_chunks):
            tile_copies[i].wait()

            def step(k, carry):
                high, low = split(raw[k])
                tile_hi[k] = high
                tile_lo[k] = low
                return carry

            lax.fori_loop(i * chunk, (i + 1) * chunk, step, 0)

    def split_blocks(n, source, target):
        def step(i, carry):
            for j in range(CAP):
                high, low = split(source[i, j])
                target[i * CAP + j, 0:nv] = high
                target[i * CAP + j, nv:2 * nv] = low
            return carry

        lax.fori_loop(0, n, step, 0)

    def multiply(line, blocks, pick, n, out, dot):
        width = 4 if slots % 4 == 0 else 1

        def step(g, carry):
            for u in range(width):
                k = g * width + u
                x = blocks[jnp.maximum(tab_s[line, 0, k], 0)]
                wide = dot(x, tile_hi[k])
                z = wide[0:nv] + wide[nv:2 * nv] + dot(x[0:nv], tile_lo[k])
                high, low = split(z)
                z_hi[k] = high
                z_lo[k] = low
            return carry

        lax.fori_loop(0, slots // width, step, 0)
        flat = (slots * nv, TILE)
        y = dot_nn(pick[...], z_hi[...].reshape(flat)) + dot_nn(pick[...], z_lo[...].reshape(flat))
        out[...] = y.reshape(n, CAP, nv, TILE)

    exchanges = [idx_r, idx_c]

    def apply(which, first, after_rows, after_gather, after_columns):
        send_r, send_c, got_r, got_c, back_r, back_c, y_r, y_c = rounds[which][:8]
        gr_s, gc_s, br_s, bc_s, rr = rounds[which][8:]
        gather_r = Exchange("col", lambda p: send_r.at[p], lambda i: got_r.at[i], gr_s, rr.at[0])
        gather_c = Exchange("row", lambda p: send_c.at[p], lambda i: got_c.at[i], gc_s, rr.at[1])
        scatter_r = Exchange("col", lambda p: y_r.at[p], lambda i: back_r.at[i, pl.ds(0, CAP)], br_s, rr.at[2])
        scatter_c = Exchange("row", lambda p: y_c.at[p], lambda i: back_c.at[i, pl.ds(0, CAP)], bc_s, rr.at[3])
        exchanges.extend([gather_r, gather_c, scatter_r, scatter_c])

        def pack(axis, base, exchange, send, got):
            n, me, device = axes[axis]

            def one(p):
                for j in range(CAP):
                    send[p, j] = own[which, idx_s[base + p, 0, j]]
                exchange.make(p, me).start()

            each_peer(axis, one)
            for j in range(CAP):
                got[me, j] = own[which, idx_s[base + me, 0, j]]

        pack("row", n_col, gather_c, send_c, got_c)
        pack("col", 0, gather_r, send_r, got_r)
        first()
        gather_c.wait_recv()
        split_blocks(n_row, got_c, zc)
        multiply(n_row + n_col + 1, zc, pick_r, n_col, y_r, dot_nt)
        scatter_r.start()
        for j in range(CAP):
            back_r[col, j] = y_r[col, j]
        after_rows()
        gather_r.wait_recv()
        split_blocks(n_col, got_r, zr)
        after_gather(got_r, y_r)
        multiply(n_row + n_col, zr, pick_c, n_row, y_c, dot_nn)
        scatter_c.start()
        for j in range(CAP):
            back_c[row, j] = y_c[row, j]
        after_columns()
        scatter_c.wait_recv()
        scatter_r.wait_recv()
        for b in range(segb):
            total = zero_block
            for i in range(n_row):
                total = total + back_c[i, idx_s[n_col + i, 0, POS + b]]
            for i in range(n_col):
                total = total + back_r[i, idx_s[i, 0, POS + b]]
            own[which + 1, b] = total

    def setup():
        build_pick(n_row + n_col, pick_r)
        build_pick(n_row + n_col + 1, pick_c)
        split_tiles()

    nothing = lambda *unused: None
    apply(0, setup, nothing, nothing, nothing)

    corr_row = Exchange("row", lambda p: corr_1.at[row], lambda i: corr_1.at[i], c1_s, c1_r)
    corr_col = Exchange("col", lambda p: corr_2.at[col], lambda i: corr_2.at[i], c2_s, c2_r)
    gram_row = Exchange("row", lambda p: gram_1.at[row], lambda i: gram_1.at[i], g1_s, g1_r)
    gram_col = Exchange("col", lambda p: gram_2.at[col], lambda i: gram_2.at[i], g2_s, g2_r)
    exchanges.extend([corr_row, corr_col, gram_row, gram_col])

    def total_of(ref, n):
        total = ref[0]
        for i in range(1, n):
            total = total + ref[i]
        return total

    def correlate():
        total = jnp.zeros((2 * nv, 2 * nv), F32)
        for b in range(segb):
            both = jnp.concatenate([own[0, b], own[1, b]], axis=0)
            total = total + dot_nt(both, both, EXACT)
        corr_1[row, :, 0:2 * nv] = total
        corr_row.start()

    def correlate_on():
        corr_row.wait_recv()
        corr_2[col] = total_of(corr_1, n_row)
        corr_col.start()

    def gram_terms(got_r, y_r):
        def step(i, total):
            for j in range(CAP):
                total = total + dot_nt(got_r[i, j], y_r[i, j], EXACT)
            return total

        gram_1[row, :, 0:nv] = lax.fori_loop(0, n_col, step, jnp.zeros((nv, nv), F32))
        gram_row.start()

    answers = []

    def solve():
        gram_row.wait_recv()
        gram_2[col] = total_of(gram_1, n_row)
        gram_col.start()
        corr_col.wait_recv()
        sums = total_of(corr_2, n_col)
        lanes = sums.shape[1]
        m = sums[0:nv]
        line = lax.broadcasted_iota(jnp.int32, (nv, lanes), 0)
        lane = lax.broadcasted_iota(jnp.int32, (nv, lanes), 1)
        for i in range(nv):
            pivot_row = m[i:i + 1, :] / m[i:i + 1, i:i + 1]
            m = jnp.where(line == i, pivot_row, m - m[:, i:i + 1] * pivot_row)
        second = jnp.where(lane == line + nv, 1.0, 0.0).astype(F32)
        coeffs_t = dot_nt(second, m, EXACT)
        proj = dot_nt(sums[0:nv], second, EXACT)
        squares = dot_nt(sums[nv:2 * nv], second, EXACT)
        answers.extend([coeffs_t, proj, squares])
        for b in range(segb):
            residual[:, b * TILE:(b + 1) * TILE] = own[1, b] - dot_nn(coeffs_t, own[0, b], EXACT)

    apply(1, correlate, correlate_on, gram_terms, solve)
    coeffs_t, proj, squares = answers
    for b in range(segb):
        image[:, b * TILE:(b + 1) * TILE] = own[2, b] - dot_nn(coeffs_t, own[1, b], EXACT)
    gram_col.wait_recv()
    half = total_of(gram_2, n_col)[:, 0:nv]
    eye = jnp.where(
        lax.broadcasted_iota(jnp.int32, (nv, nv), 0) == lax.broadcasted_iota(jnp.int32, (nv, nv), 1),
        1.0, 0.0,
    ).astype(F32)
    whole = half + dot_nt(eye, half, EXACT)
    whole = whole - dot_nn(coeffs_t, squares, EXACT) - dot_nt(squares, coeffs_t, EXACT)
    whole = whole + dot_nt(dot_nn(coeffs_t, proj, EXACT), coeffs_t, EXACT)
    gram[...] = whole / order
    for e in exchanges:
        e.wait_send()


def per_device(n_row, n_col, vectors, tiles, tile_rows, tile_cols, counts):
    nv, width = vectors.shape
    segb = width // TILE
    slots = tiles.shape[2]
    lines = n_row + n_col + 2
    smem = pl.BlockSpec(memory_space=pltpu.SMEM)
    vmem = pl.BlockSpec(memory_space=pltpu.VMEM)
    table = pl.pallas_call(
        functools.partial(prep_kernel, n_row, n_col, segb),
        out_shape=jax.ShapeDtypeStruct((lines, 1, 128), jnp.int32),
        in_specs=[smem] * 3,
        out_specs=smem,
    )(tile_rows, tile_cols, counts)
    dma = pltpu.SemaphoreType.DMA
    rb, cb = (n_col, CAP, nv, TILE), (n_row, CAP, nv, TILE)
    most = max(n_row, n_col)
    one_round = [
        pltpu.VMEM(rb, F32), pltpu.VMEM(cb, F32), pltpu.VMEM(rb, F32), pltpu.VMEM(cb, F32),
        pltpu.VMEM((n_col, CAP + 1, nv, TILE), F32), pltpu.VMEM((n_row, CAP + 1, nv, TILE), F32),
        pltpu.VMEM(rb, F32), pltpu.VMEM(cb, F32),
        dma((n_col,)), dma((n_row,)), dma((n_col,)), dma((n_row,)), dma((4, most)),
    ]
    scratch = [
        pltpu.VMEM((slots, TILE, TILE), F32),
        pltpu.VMEM((slots, TILE, TILE), BF16),
        pltpu.VMEM((slots, TILE, TILE), BF16),
        pltpu.VMEM((n_col * CAP * nv, slots * nv), BF16),
        pltpu.VMEM((n_row * CAP * nv, slots * nv), BF16),
        pltpu.VMEM((slots, nv, TILE), BF16),
        pltpu.VMEM((slots, nv, TILE), BF16),
        pltpu.VMEM((n_row + n_col, 1, 128), jnp.int32),
        pltpu.SMEM((n_row + n_col, 1, 128), jnp.int32),
        pltpu.VMEM((3, segb, nv, TILE), F32),
        pltpu.VMEM((n_col * CAP, 2 * nv, TILE), BF16),
        pltpu.VMEM((n_row * CAP, 2 * nv, TILE), BF16),
        pltpu.VMEM((n_row, 2 * nv, 128), F32),
        pltpu.VMEM((n_col, 2 * nv, 128), F32),
        pltpu.VMEM((n_row, nv, 128), F32),
        pltpu.VMEM((n_col, nv, 128), F32),
        dma((slots,)),
        dma(()),
        *one_round,
        *one_round,
        dma((n_col,)), dma((n_col,)), dma((n_row,)), dma((n_row,)),
        dma((n_row,)), dma((n_row,)), dma((n_col,)), dma((n_col,)),
        dma((n_row,)), dma((n_row,)), dma((n_col,)), dma((n_col,)),
    ]
    order = width * n_row * n_col
    return pl.pallas_call(
        functools.partial(main_kernel, n_row, n_col, segb, order),
        out_shape=(
            jax.ShapeDtypeStruct((nv, width), F32),
            jax.ShapeDtypeStruct((nv, width), F32),
            jax.ShapeDtypeStruct((nv, nv), F32),
        ),
        in_specs=[smem, vmem, vmem, pl.BlockSpec(memory_space=pl.ANY)],
        out_specs=(vmem, vmem, vmem),
        scratch_shapes=scratch,
        compiler_params=pltpu.CompilerParams(
            collective_id=0, has_side_effects=True, vmem_limit_bytes=52 * 2**20
        ),
    )(table, table, vectors, tiles)


def solution(mesh):
    in_specs = (
        P(None, ("row", "col")),
        P("row", "col", None, None, None),
        P("row", "col", None),
        P("row", "col", None),
        P("row", "col"),
    )
    out_specs = (P(None, ("row", "col")), P(None, ("row", "col")), P())
    body = functools.partial(per_device, mesh.shape["row"], mesh.shape["col"])
    return jax.shard_map(body, mesh=mesh, in_specs=in_specs, out_specs=out_specs, check_vma=False)
```

```python
import functools

import jax
import jax.numpy as jnp
from jax import lax
from jax.experimental import pallas as pl
from jax.experimental.pallas import tpu as pltpu
from jax.sharding import PartitionSpec as P

TILE = 256
CAP = 3
NEED = 8
MESH = pl.DeviceIdType.MESH
F32 = jnp.float32
BF16 = jnp.bfloat16
EXACT = lax.Precision.HIGHEST


def dot_nt(a, b, precision=None):
    return lax.dot_general(
        a, b, (((1,), (1,)), ((), ())), precision=precision, preferred_element_type=F32
    )


def dot_nn(a, b, precision=None):
    return lax.dot_general(
        a, b, (((1,), (0,)), ((), ())), precision=precision, preferred_element_type=F32
    )


def split(x):
    high = x.astype(BF16)
    return high, (x - high.astype(F32)).astype(BF16)


def main_kernel(n_row, n_col, segb, order, *refs):
    (rows, cols, count, vec, tiles, residual, image, gram) = refs[:8]
    refs = refs[8:]
    (
        raw, tile_hi, tile_lo, pick_r, pick_c, z_hi, z_lo, idx_v, idx_s, own,
        zr, zc, corr_1, corr_2, gram_1, gram_2, tab_v, tab_s, slot_s, out_v, later, small,
        tile_sem, idx_sem, tab_sem, vec_sem, out_sem,
    ) = refs[:27]
    rounds = [refs[27:40], refs[40:53]]
    (ir_s, ir_r, ic_s, ic_r, c1_s, c1_r, c2_s, c2_r, g1_s, g1_r, g2_s, g2_r) = refs[53:65]
    nv = vec.shape[0]
    slots = raw.shape[0]
    row = lax.axis_index("row")
    col = lax.axis_index("col")
    axes = {
        "row": (n_row, row, lambda p: (p, col)),
        "col": (n_col, col, lambda p: (row, p)),
    }

    def each_peer(axis, body):
        n, me, device = axes[axis]

        def step(d, carry):
            body(lax.rem(me + d, n))
            return carry

        lax.fori_loop(1, n, step, 0)

    def copy(axis, source, target, send, recv, p, slot):
        return pltpu.make_async_remote_copy(
            src_ref=source, dst_ref=target, send_sem=send.at[p], recv_sem=recv.at[slot],
            device_id=axes[axis][2](p), device_id_type=MESH,
        )

    class Exchange:
        def __init__(self, axis, source, target, send, recv):
            self.axis, self.source, self.target = axis, source, target
            self.send, self.recv = send, recv

        def make(self, p, slot):
            return copy(self.axis, self.source(p), self.target(slot), self.send, self.recv, p, slot)

        def start(self):
            me = axes[self.axis][1]
            each_peer(self.axis, lambda p: self.make(p, me).start())

        def wait_recv(self):
            each_peer(self.axis, lambda p: self.make(p, p).wait_recv())

        def wait_send(self):
            me = axes[self.axis][1]
            each_peer(self.axis, lambda p: self.make(p, me).wait_send())

    chunk = 8 if slots % 8 == 0 else 1
    n_chunks = slots // chunk
    tile_copies = [
        pltpu.make_async_copy(
            tiles.at[0, 0, pl.ds(i * chunk, chunk)], raw.at[pl.ds(i * chunk, chunk)], tile_sem.at[i]
        )
        for i in range(n_chunks)
    ]
    vec_copies = [
        pltpu.make_async_copy(vec.at[:, pl.ds(b * TILE, TILE)], own.at[0, b], vec_sem.at[b])
        for b in range(segb)
    ]
    for c in vec_copies + tile_copies:
        c.start()

    barrier = pltpu.get_barrier_semaphore()
    for axis in ("row", "col"):
        device = axes[axis][2]
        each_peer(
            axis,
            lambda p: pl.semaphore_signal(
                barrier, inc=1, device_id=device(p), device_id_type=MESH
            ),
        )

    lane = lax.broadcasted_iota(jnp.int32, (8, 128), 1)
    line = lax.broadcasted_iota(jnp.int32, (8, 128), 0)
    live_count = count[0, 0]
    seg = jnp.zeros((8, 128), jnp.int32)
    for i in range(1, 128 // segb + 1):
        seg = seg + (lane >= i * segb).astype(jnp.int32)
    block = lane - seg * segb

    def touch(g, named):
        for u in range(unroll):
            k = g * unroll + u
            live = k < live_count
            which = jnp.where(
                line == 0, jnp.where(live, rows[0, 0, k], -1), jnp.where(live, cols[0, 0, k], -1)
            )
            named = jnp.where(lane == which, 1, named)
        return named

    unroll = 8 if slots % 8 == 0 else 1
    named = lax.fori_loop(0, slots // unroll, touch, jnp.zeros((8, 128), jnp.int32))
    rank = jnp.zeros((8, 128), jnp.int32)
    for d in range(1, segb):
        rank = rank + jnp.where(block >= d, pltpu.roll(named, d, 1), 0)
    need = jnp.zeros((8, 128), jnp.int32)
    for d in range(segb):
        moved = jnp.where((named > 0) & (block - rank == d), block, 0)
        need = need + (pltpu.roll(moved, 128 - d, 1) if d else moved)
    message = jnp.where(named > 0, rank, CAP) + NEED * need
    place = seg * CAP + rank
    tab_v[0] = message[0:1]
    tab_v[1] = message[1:2]
    tab_v[2] = place[0:1]
    tab_v[3] = place[1:2]
    idx_v[col] = message[0:1]
    idx_v[n_col + row] = message[1:2]
    to_tab = pltpu.make_async_copy(tab_v, tab_s, tab_sem)
    to_tab.start()
    corr_1[...] = jnp.zeros_like(corr_1)
    corr_2[...] = jnp.zeros_like(corr_2)
    gram_1[...] = jnp.zeros_like(gram_1)
    gram_2[...] = jnp.zeros_like(gram_2)
    zero_block = jnp.zeros((nv, TILE), F32)
    for r in rounds:
        back_r, back_c = r[4], r[5]
        for i in range(n_col):
            back_r[i, CAP] = zero_block
        for i in range(n_row):
            back_c[i, CAP] = zero_block
    pl.semaphore_wait(barrier, n_row + n_col - 2)

    idx_r = Exchange("col", lambda p: tab_v.at[0], lambda i: idx_v.at[i], ir_s, ir_r)
    idx_c = Exchange("row", lambda p: tab_v.at[1], lambda i: idx_v.at[n_col + i], ic_s, ic_r)
    idx_r.start()
    idx_c.start()
    to_tab.wait()

    def place_slots(k, carry):
        live = k < live_count
        slot_s[0, k] = jnp.where(live, tab_s[2, 0, rows[0, 0, k]], -1)
        slot_s[1, k] = jnp.where(live, tab_s[3, 0, cols[0, 0, k]], -1)
        return carry

    lax.fori_loop(0, slots, place_slots, 0)

    def build_pick(line, pick):
        n, wide = pick.shape
        lane = lax.broadcasted_iota(jnp.int32, (8, wide), 1)
        slot_of, vector_of = lane // nv, lane % nv

        def step(k, carry):
            return jnp.where(slot_of == k, vector_of + nv * slot_s[line, k], carry)

        wanted = lax.fori_loop(0, slots, step, jnp.full((8, wide), -1, jnp.int32))[0:1]
        part = CAP * nv

        def fill(i, carry):
            at = lax.broadcasted_iota(jnp.int32, (part, wide), 0) + i * part
            pick[pl.ds(pl.multiple_of(i * part, part), part), :] = jnp.where(
                at == wanted, 1.0, 0.0
            ).astype(BF16)
            return carry

        lax.fori_loop(0, n // part, fill, 0)

    build_pick(0, pick_r)
    build_pick(1, pick_c)
    for c in vec_copies:
        c.wait()
    idx_c.wait_recv()
    idx_r.wait_recv()
    to_smem = pltpu.make_async_copy(idx_v, idx_s, idx_sem)
    to_smem.start()
    to_smem.wait()

    def needed(i, seg_of, j):
        return lax.shift_right_logical(idx_s[i, 0, seg_of * segb + j], 3)

    def position(i, seg_of, b):
        return idx_s[i, 0, seg_of * segb + b] & (NEED - 1)

    def split_blocks(n, source, target):
        def step(i, carry):
            for j in range(CAP):
                high, low = split(source[i, j])
                target[i * CAP + j, 0:nv] = high
                target[i * CAP + j, nv:2 * nv] = low
            return carry

        lax.fori_loop(0, n, step, 0)

    def multiply(line, blocks, pick, n, out, dot, fresh):
        width = 4 if chunk % 4 == 0 else 1

        def step(g, carry):
            for u in range(width):
                k = g * width + u
                x = blocks[jnp.maximum(slot_s[line, k], 0)]
                if fresh:
                    t_hi, t_lo = split(raw[k])
                    tile_hi[k] = t_hi
                    tile_lo[k] = t_lo
                else:
                    t_hi, t_lo = tile_hi[k], tile_lo[k]
                wide = dot(x, t_hi)
                z = wide[0:nv] + wide[nv:2 * nv] + dot(x[0:nv], t_lo)
                high, low = split(z)
                z_hi[k] = high
                z_lo[k] = low
            return carry

        per = chunk // width
        if fresh:
            for i in range(n_chunks):
                tile_copies[i].wait()
                lax.fori_loop(i * per, (i + 1) * per, step, 0)
        else:
            lax.fori_loop(0, n_chunks * per, step, 0)
        flat = (slots * nv, TILE)
        y = dot_nn(pick[...], z_hi[...].reshape(flat)) + dot_nn(pick[...], z_lo[...].reshape(flat))
        out[...] = y.reshape(n, CAP, nv, TILE)

    exchanges = [idx_r, idx_c]

    def apply(which, first, after_rows, after_gather, after_columns):
        send_r, send_c, got_r, got_c, back_r, back_c, y_r, y_c = rounds[which][:8]
        gr_s, gc_s, br_s, bc_s, rr = rounds[which][8:]
        gather_r = Exchange("col", lambda p: send_r.at[p], lambda i: got_r.at[i], gr_s, rr.at[0])
        gather_c = Exchange("row", lambda p: send_c.at[p], lambda i: got_c.at[i], gc_s, rr.at[1])
        scatter_r = Exchange("col", lambda p: y_r.at[p], lambda i: back_r.at[i, pl.ds(0, CAP)], br_s, rr.at[2])
        scatter_c = Exchange("row", lambda p: y_c.at[p], lambda i: back_c.at[i, pl.ds(0, CAP)], bc_s, rr.at[3])
        exchanges.extend([gather_r, gather_c, scatter_r, scatter_c])

        def pack(axis, base, exchange, send, got):
            n, me, device = axes[axis]

            def one(p):
                for j in range(CAP):
                    send[p, j] = own[which, needed(base + p, me, j)]
                exchange.make(p, me).start()

            each_peer(axis, one)
            for j in range(CAP):
                got[me, j] = own[which, needed(base + me, me, j)]

        pack("row", n_col, gather_c, send_c, got_c)
        pack("col", 0, gather_r, send_r, got_r)
        first()
        gather_c.wait_recv()
        split_blocks(n_row, got_c, zc)
        multiply(1, zc, pick_r, n_col, y_r, dot_nt, which == 0)
        scatter_r.start()
        for j in range(CAP):
            back_r[col, j] = y_r[col, j]
        after_rows()
        gather_r.wait_recv()
        split_blocks(n_col, got_r, zr)
        after_gather(y_r)
        multiply(0, zr, pick_c, n_row, y_c, dot_nn, False)
        scatter_c.start()
        for j in range(CAP):
            back_c[row, j] = y_c[row, j]
        after_columns()
        scatter_c.wait_recv()
        scatter_r.wait_recv()
        for b in range(segb):
            total = zero_block
            for i in range(n_row):
                total = total + back_c[i, position(n_col + i, row, b)]
            for i in range(n_col):
                total = total + back_r[i, position(i, col, b)]
            own[which + 1, b] = total

    def own_correlation():
        total = jnp.zeros((nv, nv), F32)
        for b in range(segb):
            total = total + dot_nt(own[0, b], own[0, b], EXACT)
        small[0, :, 0:nv] = total

    nothing = lambda *unused: None
    apply(0, nothing, own_correlation, nothing, nothing)

    corr_row = Exchange("row", lambda p: corr_1.at[row], lambda i: corr_1.at[i], c1_s, c1_r)
    corr_col = Exchange("col", lambda p: corr_2.at[col], lambda i: corr_2.at[i], c2_s, c2_r)
    gram_row = Exchange("row", lambda p: gram_1.at[row], lambda i: gram_1.at[i], g1_s, g1_r)
    gram_col = Exchange("col", lambda p: gram_2.at[col], lambda i: gram_2.at[i], g2_s, g2_r)
    exchanges.extend([corr_row, corr_col, gram_row, gram_col])

    def total_of(ref, n):
        total = ref[0]
        for i in range(1, n):
            total = total + ref[i]
        return total

    def fold(total, n):
        return total[0:n, 0:n] + total[0:n, n:2 * n] + total[n:2 * n, 0:n] + total[n:2 * n, n:2 * n]

    def correlate():
        total = jnp.zeros((4 * nv, 4 * nv), F32)
        for b in range(segb):
            both = jnp.concatenate(split(jnp.concatenate([own[0, b], own[1, b]], axis=0)), axis=0)
            total = total + dot_nt(both, both)
        corr_1[row, :, 0:2 * nv] = fold(total, 2 * nv)
        corr_1[row, 0:nv, 0:nv] = small[0, :, 0:nv]
        corr_row.start()

    def correlate_on():
        corr_row.wait_recv()
        corr_2[col] = total_of(corr_1, n_row)
        corr_col.start()

    eye = jnp.where(
        lax.broadcasted_iota(jnp.int32, (nv, nv), 0) == lax.broadcasted_iota(jnp.int32, (nv, nv), 1),
        1.0, 0.0,
    ).astype(F32)

    def gram_terms(y_r):
        def step(i, total):
            for j in range(CAP):
                y = jnp.concatenate(split(y_r[i, j]), axis=0)
                total = total + dot_nt(zr[i * CAP + j], y)
            return total

        total = lax.fori_loop(0, n_col, step, jnp.zeros((2 * nv, 2 * nv), F32))
        half = fold(total, nv)
        gram_1[row, :, 0:nv] = half + dot_nt(eye, half, EXACT)
        gram_row.start()

    def solve():
        gram_row.wait_recv()
        gram_2[col] = total_of(gram_1, n_row)
        gram_col.start()
        corr_col.wait_recv()
        sums = total_of(corr_2, n_col)
        lanes = sums.shape[1]
        m = sums[0:nv]
        line = lax.broadcasted_iota(jnp.int32, (nv, lanes), 0)
        lane = lax.broadcasted_iota(jnp.int32, (nv, lanes), 1)
        for i in range(nv):
            pivot_row = m[i:i + 1, :] / m[i:i + 1, i:i + 1]
            m = jnp.where(line == i, pivot_row, m - m[:, i:i + 1] * pivot_row)
        second = jnp.where(lane == line + nv, 1.0, 0.0).astype(F32)
        coeffs_t = dot_nt(second, m, EXACT)
        proj = dot_nt(sums[0:nv], second, EXACT)
        squares = dot_nt(sums[nv:2 * nv], second, EXACT)
        for b in range(segb):
            out_v[:, b * TILE:(b + 1) * TILE] = own[1, b] - dot_nn(coeffs_t, own[0, b], EXACT)
        out_copy.start()
        for b in range(segb):
            later[b] = dot_nn(coeffs_t, own[1, b], EXACT)
        rest = dot_nt(dot_nn(coeffs_t, proj, EXACT), coeffs_t, EXACT)
        rest = rest - dot_nn(coeffs_t, squares, EXACT) - dot_nt(squares, coeffs_t, EXACT)
        small[1, :, 0:nv] = rest

    out_copy = pltpu.make_async_copy(out_v, residual, out_sem)
    apply(1, correlate, correlate_on, gram_terms, solve)
    for b in range(segb):
        image[:, b * TILE:(b + 1) * TILE] = own[2, b] - later[b]
    gram_col.wait_recv()
    gram[...] = (total_of(gram_2, n_col)[:, 0:nv] + small[1, :, 0:nv]) / order
    out_copy.wait()
    for e in exchanges:
        e.wait_send()


def per_device(n_row, n_col, vectors, tiles, tile_rows, tile_cols, counts):
    nv, width = vectors.shape
    segb = width // TILE
    slots = tiles.shape[2]
    smem = pl.BlockSpec(memory_space=pltpu.SMEM)
    vmem = pl.BlockSpec(memory_space=pltpu.VMEM)
    anywhere = pl.BlockSpec(memory_space=pl.ANY)
    dma = pltpu.SemaphoreType.DMA
    rb, cb = (n_col, CAP, nv, TILE), (n_row, CAP, nv, TILE)
    most = max(n_row, n_col)
    one_round = [
        pltpu.VMEM(rb, F32), pltpu.VMEM(cb, F32), pltpu.VMEM(rb, F32), pltpu.VMEM(cb, F32),
        pltpu.VMEM((n_col, CAP + 1, nv, TILE), F32), pltpu.VMEM((n_row, CAP + 1, nv, TILE), F32),
        pltpu.VMEM(rb, F32), pltpu.VMEM(cb, F32),
        dma((n_col,)), dma((n_row,)), dma((n_col,)), dma((n_row,)), dma((4, most)),
    ]
    scratch = [
        pltpu.VMEM((slots, TILE, TILE), F32),
        pltpu.VMEM((slots, TILE, TILE), BF16),
        pltpu.VMEM((slots, TILE, TILE), BF16),
        pltpu.VMEM((n_col * CAP * nv, slots * nv), BF16),
        pltpu.VMEM((n_row * CAP * nv, slots * nv), BF16),
        pltpu.VMEM((slots, nv, TILE), BF16),
        pltpu.VMEM((slots, nv, TILE), BF16),
        pltpu.VMEM((n_row + n_col, 1, 128), jnp.int32),
        pltpu.SMEM((n_row + n_col, 1, 128), jnp.int32),
        pltpu.VMEM((3, segb, nv, TILE), F32),
        pltpu.VMEM((n_col * CAP, 2 * nv, TILE), BF16),
        pltpu.VMEM((n_row * CAP, 2 * nv, TILE), BF16),
        pltpu.VMEM((n_row, 2 * nv, 128), F32),
        pltpu.VMEM((n_col, 2 * nv, 128), F32),
        pltpu.VMEM((n_row, nv, 128), F32),
        pltpu.VMEM((n_col, nv, 128), F32),
        pltpu.VMEM((4, 1, 128), jnp.int32),
        pltpu.SMEM((4, 1, 128), jnp.int32),
        pltpu.SMEM((2, slots), jnp.int32),
        pltpu.VMEM((nv, width), F32),
        pltpu.VMEM((segb, nv, TILE), F32),
        pltpu.VMEM((2, nv, 128), F32),
        dma((slots,)),
        dma(()),
        dma(()),
        dma((segb,)),
        dma(()),
        *one_round,
        *one_round,
        dma((n_col,)), dma((n_col,)), dma((n_row,)), dma((n_row,)),
        dma((n_row,)), dma((n_row,)), dma((n_col,)), dma((n_col,)),
        dma((n_row,)), dma((n_row,)), dma((n_col,)), dma((n_col,)),
    ]
    order = width * n_row * n_col
    return pl.pallas_call(
        functools.partial(main_kernel, n_row, n_col, segb, order),
        out_shape=(
            jax.ShapeDtypeStruct((nv, width), F32),
            jax.ShapeDtypeStruct((nv, width), F32),
            jax.ShapeDtypeStruct((nv, nv), F32),
        ),
        in_specs=[smem, smem, smem, anywhere, anywhere],
        out_specs=(anywhere, vmem, vmem),
        scratch_shapes=scratch,
        compiler_params=pltpu.CompilerParams(
            collective_id=0, has_side_effects=True, vmem_limit_bytes=52 * 2**20
        ),
    )(tile_rows, tile_cols, counts, vectors, tiles)


def solution(mesh):
    in_specs = (
        P(None, ("row", "col")),
        P("row", "col", None, None, None),
        P("row", "col", None),
        P("row", "col", None),
        P("row", "col"),
    )
    out_specs = (P(None, ("row", "col")), P(None, ("row", "col")), P())
    body = functools.partial(per_device, mesh.shape["row"], mesh.shape["col"])
    return jax.shard_map(body, mesh=mesh, in_specs=in_specs, out_specs=out_specs, check_vma=False)
```

```python
import functools

import jax
import jax.numpy as jnp
from jax import lax
from jax.experimental import pallas as pl
from jax.experimental.pallas import tpu as pltpu
from jax.sharding import PartitionSpec as P

TILE = 256
CAP = 3
NEED = 8
MESH = pl.DeviceIdType.MESH
F32 = jnp.float32
BF16 = jnp.bfloat16
EXACT = lax.Precision.HIGHEST


def dot_nt(a, b, precision=None):
    return lax.dot_general(
        a, b, (((1,), (1,)), ((), ())), precision=precision, preferred_element_type=F32
    )


def dot_nn(a, b, precision=None):
    return lax.dot_general(
        a, b, (((1,), (0,)), ((), ())), precision=precision, preferred_element_type=F32
    )


def split(x):
    high = x.astype(BF16)
    return high, (x - high.astype(F32)).astype(BF16)


def main_kernel(n_row, n_col, segb, order, *refs):
    (rows, cols, count, vec, tiles, residual, image, gram) = refs[:8]
    refs = refs[8:]
    (
        raw, tile_hi, tile_lo, pick_r, pick_c, z_hi, z_lo, idx_v, idx_s, own,
        zr, zc, corr_1, corr_2, gram_1, gram_2, tab_v, tab_s, slot_s, out_v, later, small,
        tile_sem, idx_sem, tab_sem, vec_sem, out_sem,
    ) = refs[:27]
    rounds = [refs[27:40], refs[40:53]]
    (ir_s, ir_r, ic_s, ic_r, c1_s, c1_r, c2_s, c2_r, g1_s, g1_r, g2_s, g2_r) = refs[53:65]
    nv = vec.shape[0]
    slots = raw.shape[0]
    row = lax.axis_index("row")
    col = lax.axis_index("col")
    axes = {
        "row": (n_row, row, lambda p: (p, col)),
        "col": (n_col, col, lambda p: (row, p)),
    }

    def each_peer(axis, body):
        n, me, device = axes[axis]

        def step(d, carry):
            body(lax.rem(me + d, n))
            return carry

        lax.fori_loop(1, n, step, 0)

    def copy(axis, source, target, send, recv, p, slot):
        return pltpu.make_async_remote_copy(
            src_ref=source, dst_ref=target, send_sem=send.at[p], recv_sem=recv.at[slot],
            device_id=axes[axis][2](p), device_id_type=MESH,
        )

    class Exchange:
        def __init__(self, axis, source, target, send, recv):
            self.axis, self.source, self.target = axis, source, target
            self.send, self.recv = send, recv

        def make(self, p, slot):
            return copy(self.axis, self.source(p), self.target(slot), self.send, self.recv, p, slot)

        def start(self):
            me = axes[self.axis][1]
            each_peer(self.axis, lambda p: self.make(p, me).start())

        def wait_recv(self):
            each_peer(self.axis, lambda p: self.make(p, p).wait_recv())

        def wait_send(self):
            me = axes[self.axis][1]
            each_peer(self.axis, lambda p: self.make(p, me).wait_send())

    chunk = 8 if slots % 8 == 0 else 1
    n_chunks = slots // chunk
    tile_copies = [
        pltpu.make_async_copy(
            tiles.at[0, 0, pl.ds(i * chunk, chunk)], raw.at[pl.ds(i * chunk, chunk)], tile_sem.at[i]
        )
        for i in range(n_chunks)
    ]
    vec_copies = [
        pltpu.make_async_copy(vec.at[:, pl.ds(b * TILE, TILE)], own.at[0, b], vec_sem.at[b])
        for b in range(segb)
    ]
    for c in vec_copies + tile_copies:
        c.start()

    barrier = pltpu.get_barrier_semaphore()
    for axis in ("row", "col"):
        device = axes[axis][2]
        each_peer(
            axis,
            lambda p: pl.semaphore_signal(
                barrier, inc=1, device_id=device(p), device_id_type=MESH
            ),
        )

    lane = lax.broadcasted_iota(jnp.int32, (8, 128), 1)
    line = lax.broadcasted_iota(jnp.int32, (8, 128), 0)
    live_count = count[0, 0]
    seg = jnp.zeros((8, 128), jnp.int32)
    for i in range(1, 128 // segb + 1):
        seg = seg + (lane >= i * segb).astype(jnp.int32)
    block = lane - seg * segb

    def touch(g, named):
        for u in range(unroll):
            k = g * unroll + u
            live = k < live_count
            which = jnp.where(
                line == 0, jnp.where(live, rows[0, 0, k], -1), jnp.where(live, cols[0, 0, k], -1)
            )
            named = jnp.where(lane == which, 1, named)
        return named

    unroll = 8 if slots % 8 == 0 else 1
    named = lax.fori_loop(0, slots // unroll, touch, jnp.zeros((8, 128), jnp.int32))
    rank = jnp.zeros((8, 128), jnp.int32)
    for d in range(1, segb):
        rank = rank + jnp.where(block >= d, pltpu.roll(named, d, 1), 0)
    need = jnp.zeros((8, 128), jnp.int32)
    for d in range(segb):
        moved = jnp.where((named > 0) & (block - rank == d), block, 0)
        need = need + (pltpu.roll(moved, 128 - d, 1) if d else moved)
    message = jnp.where(named > 0, rank, CAP) + NEED * need
    place = seg * CAP + rank
    tab_v[0] = message[0:1]
    tab_v[1] = message[1:2]
    tab_v[2] = place[0:1]
    tab_v[3] = place[1:2]
    idx_v[col] = message[0:1]
    idx_v[n_col + row] = message[1:2]
    to_tab = pltpu.make_async_copy(tab_v, tab_s, tab_sem)
    to_tab.start()
    corr_1[...] = jnp.zeros_like(corr_1)
    corr_2[...] = jnp.zeros_like(corr_2)
    gram_1[...] = jnp.zeros_like(gram_1)
    gram_2[...] = jnp.zeros_like(gram_2)
    zero_block = jnp.zeros((nv, TILE), F32)
    for r in rounds:
        back_r, back_c = r[4], r[5]
        for i in range(n_col):
            back_r[i, CAP] = zero_block
        for i in range(n_row):
            back_c[i, CAP] = zero_block
    pl.semaphore_wait(barrier, n_row + n_col - 2)

    idx_r = Exchange("col", lambda p: tab_v.at[0], lambda i: idx_v.at[i], ir_s, ir_r)
    idx_c = Exchange("row", lambda p: tab_v.at[1], lambda i: idx_v.at[n_col + i], ic_s, ic_r)
    idx_r.start()
    idx_c.start()
    to_tab.wait()

    def place_slots(k, carry):
        live = k < live_count
        slot_s[0, k] = jnp.where(live, tab_s[2, 0, rows[0, 0, k]], -1)
        slot_s[1, k] = jnp.where(live, tab_s[3, 0, cols[0, 0, k]], -1)
        return carry

    lax.fori_loop(0, slots, place_slots, 0)

    def build_pick(line, pick):
        n, wide = pick.shape
        lane = lax.broadcasted_iota(jnp.int32, (8, wide), 1)
        slot_of, vector_of = lane // nv, lane % nv

        def step(k, carry):
            return jnp.where(slot_of == k, vector_of + nv * slot_s[line, k], carry)

        wanted = lax.fori_loop(0, slots, step, jnp.full((8, wide), -1, jnp.int32))[0:1]
        part = CAP * nv

        def fill(i, carry):
            at = lax.broadcasted_iota(jnp.int32, (part, wide), 0) + i * part
            pick[pl.ds(pl.multiple_of(i * part, part), part), :] = jnp.where(
                at == wanted, 1.0, 0.0
            ).astype(BF16)
            return carry

        lax.fori_loop(0, n // part, fill, 0)

    build_pick(0, pick_r)
    build_pick(1, pick_c)
    for c in vec_copies:
        c.wait()
    idx_c.wait_recv()
    idx_r.wait_recv()
    to_smem = pltpu.make_async_copy(idx_v, idx_s, idx_sem)
    to_smem.start()
    to_smem.wait()

    def needed(i, seg_of, j):
        return lax.shift_right_logical(idx_s[i, 0, seg_of * segb + j], 3)

    def position(i, seg_of, b):
        return idx_s[i, 0, seg_of * segb + b] & (NEED - 1)

    def split_blocks(n, source, target):
        def step(i, carry):
            for j in range(CAP):
                high, low = split(source[i, j])
                target[i * CAP + j, 0:nv] = high
                target[i * CAP + j, nv:2 * nv] = low
            return carry

        lax.fori_loop(0, n, step, 0)

    def multiply(line, blocks, pick, n, out, dot, fresh):
        width = chunk

        def step(g, carry):
            for u in range(width):
                k = g * width + u
                x = blocks[jnp.maximum(slot_s[line, k], 0)]
                if fresh:
                    t_hi, t_lo = split(raw[k])
                    tile_hi[k] = t_hi
                    tile_lo[k] = t_lo
                else:
                    t_hi, t_lo = tile_hi[k], tile_lo[k]
                wide = dot(x, t_hi)
                z = wide[0:nv] + wide[nv:2 * nv] + dot(x[0:nv], t_lo)
                high, low = split(z)
                z_hi[k] = high
                z_lo[k] = low
            return carry

        per = chunk // width
        if fresh:
            for i in range(n_chunks):
                tile_copies[i].wait()
                lax.fori_loop(i * per, (i + 1) * per, step, 0)
        else:
            lax.fori_loop(0, n_chunks * per, step, 0)
        flat = (slots * nv, TILE)
        y = dot_nn(pick[...], z_hi[...].reshape(flat)) + dot_nn(pick[...], z_lo[...].reshape(flat))
        out[...] = y.reshape(n, CAP, nv, TILE)

    exchanges = [idx_r, idx_c]

    def apply(which, first, after_rows, after_gather, after_columns):
        send_r, send_c, got_r, got_c, back_r, back_c, y_r, y_c = rounds[which][:8]
        gr_s, gc_s, br_s, bc_s, rr = rounds[which][8:]
        gather_r = Exchange("col", lambda p: send_r.at[p], lambda i: got_r.at[i], gr_s, rr.at[0])
        gather_c = Exchange("row", lambda p: send_c.at[p], lambda i: got_c.at[i], gc_s, rr.at[1])
        scatter_r = Exchange("col", lambda p: y_r.at[p], lambda i: back_r.at[i, pl.ds(0, CAP)], br_s, rr.at[2])
        scatter_c = Exchange("row", lambda p: y_c.at[p], lambda i: back_c.at[i, pl.ds(0, CAP)], bc_s, rr.at[3])
        exchanges.extend([gather_r, gather_c, scatter_r, scatter_c])

        def pack(axis, base, exchange, send, got):
            n, me, device = axes[axis]

            def one(p):
                for j in range(CAP):
                    send[p, j] = own[which, needed(base + p, me, j)]
                exchange.make(p, me).start()

            each_peer(axis, one)
            for j in range(CAP):
                got[me, j] = own[which, needed(base + me, me, j)]

        pack("row", n_col, gather_c, send_c, got_c)
        pack("col", 0, gather_r, send_r, got_r)
        first()
        gather_c.wait_recv()
        split_blocks(n_row, got_c, zc)
        multiply(1, zc, pick_r, n_col, y_r, dot_nt, which == 0)
        scatter_r.start()
        for j in range(CAP):
            back_r[col, j] = y_r[col, j]
        after_rows()
        gather_r.wait_recv()
        split_blocks(n_col, got_r, zr)
        after_gather(y_r)
        multiply(0, zr, pick_c, n_row, y_c, dot_nn, False)
        scatter_c.start()
        for j in range(CAP):
            back_c[row, j] = y_c[row, j]
        after_columns()
        scatter_c.wait_recv()
        scatter_r.wait_recv()
        for b in range(segb):
            total = zero_block
            for i in range(n_row):
                total = total + back_c[i, position(n_col + i, row, b)]
            for i in range(n_col):
                total = total + back_r[i, position(i, col, b)]
            own[which + 1, b] = total

    def own_correlation():
        total = jnp.zeros((nv, nv), F32)
        for b in range(segb):
            total = total + dot_nt(own[0, b], own[0, b], EXACT)
        small[0, :, 0:nv] = total

    nothing = lambda *unused: None
    apply(0, nothing, own_correlation, nothing, nothing)

    corr_row = Exchange("row", lambda p: corr_1.at[row], lambda i: corr_1.at[i], c1_s, c1_r)
    corr_col = Exchange("col", lambda p: corr_2.at[col], lambda i: corr_2.at[i], c2_s, c2_r)
    gram_row = Exchange("row", lambda p: gram_1.at[row], lambda i: gram_1.at[i], g1_s, g1_r)
    gram_col = Exchange("col", lambda p: gram_2.at[col], lambda i: gram_2.at[i], g2_s, g2_r)
    exchanges.extend([corr_row, corr_col, gram_row, gram_col])

    def total_of(ref, n):
        total = ref[0]
        for i in range(1, n):
            total = total + ref[i]
        return total

    def fold(total, n):
        return total[0:n, 0:n] + total[0:n, n:2 * n] + total[n:2 * n, 0:n] + total[n:2 * n, n:2 * n]

    def correlate():
        total = jnp.zeros((4 * nv, 4 * nv), F32)
        for b in range(segb):
            both = jnp.concatenate(split(jnp.concatenate([own[0, b], own[1, b]], axis=0)), axis=0)
            total = total + dot_nt(both, both)
        corr_1[row, :, 0:2 * nv] = fold(total, 2 * nv)
        corr_1[row, 0:nv, 0:nv] = small[0, :, 0:nv]
        corr_row.start()

    def correlate_on():
        corr_row.wait_recv()
        corr_2[col] = total_of(corr_1, n_row)
        corr_col.start()

    eye = jnp.where(
        lax.broadcasted_iota(jnp.int32, (nv, nv), 0) == lax.broadcasted_iota(jnp.int32, (nv, nv), 1),
        1.0, 0.0,
    ).astype(F32)

    def gram_terms(y_r):
        def step(i, total):
            for j in range(CAP):
                y = jnp.concatenate(split(y_r[i, j]), axis=0)
                total = total + dot_nt(zr[i * CAP + j], y)
            return total

        total = lax.fori_loop(0, n_col, step, jnp.zeros((2 * nv, 2 * nv), F32))
        half = fold(total, nv)
        gram_1[row, :, 0:nv] = half + dot_nt(eye, half, EXACT)
        gram_row.start()

    def solve():
        gram_row.wait_recv()
        gram_2[col] = total_of(gram_1, n_row)
        gram_col.start()
        corr_col.wait_recv()
        sums = total_of(corr_2, n_col)
        lanes = sums.shape[1]
        m = sums[0:nv]
        line = lax.broadcasted_iota(jnp.int32, (nv, lanes), 0)
        lane = lax.broadcasted_iota(jnp.int32, (nv, lanes), 1)
        for i in range(nv):
            pivot_row = m[i:i + 1, :] / m[i:i + 1, i:i + 1]
            m = jnp.where(line == i, pivot_row, m - m[:, i:i + 1] * pivot_row)
        second = jnp.where(lane == line + nv, 1.0, 0.0).astype(F32)
        coeffs_t = dot_nt(second, m, EXACT)
        proj = dot_nt(sums[0:nv], second, EXACT)
        squares = dot_nt(sums[nv:2 * nv], second, EXACT)
        for b in range(segb):
            out_v[:, b * TILE:(b + 1) * TILE] = own[1, b] - dot_nn(coeffs_t, own[0, b], EXACT)
        out_copy.start()
        for b in range(segb):
            later[b] = dot_nn(coeffs_t, own[1, b], EXACT)
        rest = dot_nt(dot_nn(coeffs_t, proj, EXACT), coeffs_t, EXACT)
        rest = rest - dot_nn(coeffs_t, squares, EXACT) - dot_nt(squares, coeffs_t, EXACT)
        small[1, :, 0:nv] = rest

    out_copy = pltpu.make_async_copy(out_v, residual, out_sem)
    apply(1, correlate, correlate_on, gram_terms, solve)
    for b in range(segb):
        image[:, b * TILE:(b + 1) * TILE] = own[2, b] - later[b]
    gram_col.wait_recv()
    gram[...] = (total_of(gram_2, n_col)[:, 0:nv] + small[1, :, 0:nv]) / order
    out_copy.wait()
    for e in exchanges:
        e.wait_send()


def per_device(n_row, n_col, vectors, tiles, tile_rows, tile_cols, counts):
    nv, width = vectors.shape
    segb = width // TILE
    slots = tiles.shape[2]
    smem = pl.BlockSpec(memory_space=pltpu.SMEM)
    vmem = pl.BlockSpec(memory_space=pltpu.VMEM)
    anywhere = pl.BlockSpec(memory_space=pl.ANY)
    dma = pltpu.SemaphoreType.DMA
    rb, cb = (n_col, CAP, nv, TILE), (n_row, CAP, nv, TILE)
    most = max(n_row, n_col)
    one_round = [
        pltpu.VMEM(rb, F32), pltpu.VMEM(cb, F32), pltpu.VMEM(rb, F32), pltpu.VMEM(cb, F32),
        pltpu.VMEM((n_col, CAP + 1, nv, TILE), F32), pltpu.VMEM((n_row, CAP + 1, nv, TILE), F32),
        pltpu.VMEM(rb, F32), pltpu.VMEM(cb, F32),
        dma((n_col,)), dma((n_row,)), dma((n_col,)), dma((n_row,)), dma((4, most)),
    ]
    scratch = [
        pltpu.VMEM((slots, TILE, TILE), F32),
        pltpu.VMEM((slots, TILE, TILE), BF16),
        pltpu.VMEM((slots, TILE, TILE), BF16),
        pltpu.VMEM((n_col * CAP * nv, slots * nv), BF16),
        pltpu.VMEM((n_row * CAP * nv, slots * nv), BF16),
        pltpu.VMEM((slots, nv, TILE), BF16),
        pltpu.VMEM((slots, nv, TILE), BF16),
        pltpu.VMEM((n_row + n_col, 1, 128), jnp.int32),
        pltpu.SMEM((n_row + n_col, 1, 128), jnp.int32),
        pltpu.VMEM((3, segb, nv, TILE), F32),
        pltpu.VMEM((n_col * CAP, 2 * nv, TILE), BF16),
        pltpu.VMEM((n_row * CAP, 2 * nv, TILE), BF16),
        pltpu.VMEM((n_row, 2 * nv, 128), F32),
        pltpu.VMEM((n_col, 2 * nv, 128), F32),
        pltpu.VMEM((n_row, nv, 128), F32),
        pltpu.VMEM((n_col, nv, 128), F32),
        pltpu.VMEM((4, 1, 128), jnp.int32),
        pltpu.SMEM((4, 1, 128), jnp.int32),
        pltpu.SMEM((2, slots), jnp.int32),
        pltpu.VMEM((nv, width), F32),
        pltpu.VMEM((segb, nv, TILE), F32),
        pltpu.VMEM((2, nv, 128), F32),
        dma((slots,)),
        dma(()),
        dma(()),
        dma((segb,)),
        dma(()),
        *one_round,
        *one_round,
        dma((n_col,)), dma((n_col,)), dma((n_row,)), dma((n_row,)),
        dma((n_row,)), dma((n_row,)), dma((n_col,)), dma((n_col,)),
        dma((n_row,)), dma((n_row,)), dma((n_col,)), dma((n_col,)),
    ]
    order = width * n_row * n_col
    return pl.pallas_call(
        functools.partial(main_kernel, n_row, n_col, segb, order),
        out_shape=(
            jax.ShapeDtypeStruct((nv, width), F32),
            jax.ShapeDtypeStruct((nv, width), F32),
            jax.ShapeDtypeStruct((nv, nv), F32),
        ),
        in_specs=[smem, smem, smem, anywhere, anywhere],
        out_specs=(anywhere, vmem, vmem),
        scratch_shapes=scratch,
        compiler_params=pltpu.CompilerParams(
            collective_id=0, has_side_effects=True, vmem_limit_bytes=60 * 2**20
        ),
    )(tile_rows, tile_cols, counts, vectors, tiles)


def solution(mesh):
    in_specs = (
        P(None, ("row", "col")),
        P("row", "col", None, None, None),
        P("row", "col", None),
        P("row", "col", None),
        P("row", "col"),
    )
    out_specs = (P(None, ("row", "col")), P(None, ("row", "col")), P())
    body = functools.partial(per_device, mesh.shape["row"], mesh.shape["col"])
    return jax.shard_map(body, mesh=mesh, in_specs=in_specs, out_specs=out_specs, check_vma=False)
```

```python
import functools

import jax
import jax.numpy as jnp
from jax import lax
from jax.experimental import pallas as pl
from jax.experimental.pallas import tpu as pltpu
from jax.sharding import PartitionSpec as P

TILE = 256
CAP = 3
NEED = 8
MESH = pl.DeviceIdType.MESH
F32 = jnp.float32
BF16 = jnp.bfloat16
EXACT = lax.Precision.HIGHEST


def dot_nt(a, b, precision=None):
    return lax.dot_general(
        a, b, (((1,), (1,)), ((), ())), precision=precision, preferred_element_type=F32
    )


def dot_nn(a, b, precision=None):
    return lax.dot_general(
        a, b, (((1,), (0,)), ((), ())), precision=precision, preferred_element_type=F32
    )


def split(x):
    high = x.astype(BF16)
    return high, (x - high.astype(F32)).astype(BF16)


def iota(shape, dim):
    return lax.broadcasted_iota(jnp.int32, shape, dim)


def one_hot(condition):
    return jnp.where(condition, 1.0, 0.0).astype(F32)


def spread(n):
    per = 128 // n
    lanes = one_hot(iota((n, 128), 1) % n == iota((n, 128), 0))
    kept = one_hot(iota((n, 128), 1) // n == iota((n, 128), 0) % per)
    lines = one_hot(iota((n // per, n), 1) // per == iota((n // per, n), 0))
    back = one_hot(iota((n, n // per), 0) // per == iota((n, n // per), 1))
    return lanes, kept, lines, back


def pack_square(x):
    lanes, kept, lines, _ = spread(x.shape[0])
    return dot_nn(lines, dot_nn(x, lanes, EXACT) * kept, EXACT)


def unpack_square(x, n):
    lanes, kept, _, back = spread(n)
    return dot_nt(dot_nn(back, x, EXACT) * kept, lanes, EXACT)


def main_kernel(n_row, n_col, segb, order, *refs):
    (rows_hbm, cols_hbm, count, vec, tiles, residual, image, gram) = refs[:8]
    refs = refs[8:]
    (
        raw, tile_hi, tile_lo, pick_r, pick_c, z_hi, z_lo, idx_v, idx_s, own,
        zr, zc, corr_1, corr_2, gram_1, gram_2, tab_v, tab_s, slot_s, out_v, later, small,
        tile_sem, idx_sem, tab_sem, vec_sem, out_sem, rows, cols, list_sem,
    ) = refs[:30]
    rounds = [refs[30:43], refs[43:56]]
    (ir_s, ir_r, ic_s, ic_r, c1_s, c1_r, c2_s, c2_r, g1_s, g1_r, g2_s, g2_r) = refs[56:68]
    nv = vec.shape[0]
    slots = raw.shape[0]
    row = lax.axis_index("row")
    col = lax.axis_index("col")
    axes = {
        "row": (n_row, row, lambda p: (p, col)),
        "col": (n_col, col, lambda p: (row, p)),
    }

    def each_peer(axis, body):
        n, me, device = axes[axis]

        def step(d, carry):
            body(lax.rem(me + d, n))
            return carry

        lax.fori_loop(1, n, step, 0)

    def copy(axis, source, target, send, recv, p, slot):
        return pltpu.make_async_remote_copy(
            src_ref=source, dst_ref=target, send_sem=send.at[p], recv_sem=recv.at[slot],
            device_id=axes[axis][2](p), device_id_type=MESH,
        )

    class Exchange:
        def __init__(self, axis, source, target, send, recv):
            self.axis, self.source, self.target = axis, source, target
            self.send, self.recv = send, recv

        def make(self, p, slot):
            return copy(self.axis, self.source(p), self.target(slot), self.send, self.recv, p, slot)

        def start(self):
            me = axes[self.axis][1]
            each_peer(self.axis, lambda p: self.make(p, me).start())

        def wait_recv(self):
            each_peer(self.axis, lambda p: self.make(p, p).wait_recv())

        def wait_send(self):
            me = axes[self.axis][1]
            each_peer(self.axis, lambda p: self.make(p, me).wait_send())

    chunk = 8 if slots % 8 == 0 else 1
    n_chunks = slots // chunk
    tile_copies = [
        pltpu.make_async_copy(
            tiles.at[0, 0, pl.ds(i * chunk, chunk)], raw.at[pl.ds(i * chunk, chunk)], tile_sem.at[i]
        )
        for i in range(n_chunks)
    ]
    vec_copies = [
        pltpu.make_async_copy(vec.at[:, pl.ds(b * TILE, TILE)], own.at[0, b], vec_sem.at[b])
        for b in range(segb)
    ]
    list_copies = [
        pltpu.make_async_copy(rows_hbm, rows, list_sem.at[0]),
        pltpu.make_async_copy(cols_hbm, cols, list_sem.at[1]),
    ]
    for c in list_copies + vec_copies + tile_copies:
        c.start()

    barrier = pltpu.get_barrier_semaphore()
    for axis in ("row", "col"):
        device = axes[axis][2]
        each_peer(
            axis,
            lambda p: pl.semaphore_signal(
                barrier, inc=1, device_id=device(p), device_id_type=MESH
            ),
        )

    lane = lax.broadcasted_iota(jnp.int32, (8, 128), 1)
    line = lax.broadcasted_iota(jnp.int32, (8, 128), 0)
    live_count = count[0, 0]
    seg = jnp.zeros((8, 128), jnp.int32)
    for i in range(1, 128 // segb + 1):
        seg = seg + (lane >= i * segb).astype(jnp.int32)
    block = lane - seg * segb

    def touch(g, named):
        for u in range(unroll):
            k = g * unroll + u
            live = k < live_count
            which = jnp.where(
                line == 0, jnp.where(live, rows[0, 0, k], -1), jnp.where(live, cols[0, 0, k], -1)
            )
            named = jnp.where(lane == which, 1, named)
        return named

    unroll = 8 if slots % 8 == 0 else 1
    for c in list_copies:
        c.wait()
    named = lax.fori_loop(0, slots // unroll, touch, jnp.zeros((8, 128), jnp.int32))
    rank = jnp.zeros((8, 128), jnp.int32)
    for d in range(1, segb):
        rank = rank + jnp.where(block >= d, pltpu.roll(named, d, 1), 0)
    need = jnp.zeros((8, 128), jnp.int32)
    for d in range(segb):
        moved = jnp.where((named > 0) & (block - rank == d), block, 0)
        need = need + (pltpu.roll(moved, 128 - d, 1) if d else moved)
    message = jnp.where(named > 0, rank, CAP) + NEED * need
    place = seg * CAP + rank
    tab_v[0] = message[0:1]
    tab_v[1] = message[1:2]
    tab_v[2] = place[0:1]
    tab_v[3] = place[1:2]
    idx_v[col] = message[0:1]
    idx_v[n_col + row] = message[1:2]
    to_tab = pltpu.make_async_copy(tab_v, tab_s, tab_sem)
    to_tab.start()
    zero_block = jnp.zeros((nv, TILE), F32)
    for r in rounds:
        back_r, back_c = r[4], r[5]
        for i in range(n_col):
            back_r[i, CAP] = zero_block
        for i in range(n_row):
            back_c[i, CAP] = zero_block
    pl.semaphore_wait(barrier, n_row + n_col - 2)

    idx_r = Exchange("col", lambda p: tab_v.at[0], lambda i: idx_v.at[i], ir_s, ir_r)
    idx_c = Exchange("row", lambda p: tab_v.at[1], lambda i: idx_v.at[n_col + i], ic_s, ic_r)
    idx_r.start()
    idx_c.start()
    to_tab.wait()

    def place_slots(k, carry):
        live = k < live_count
        slot_s[0, k] = jnp.where(live, tab_s[2, 0, rows[0, 0, k]], -1)
        slot_s[1, k] = jnp.where(live, tab_s[3, 0, cols[0, 0, k]], -1)
        return carry

    lax.fori_loop(0, slots, place_slots, 0)

    def build_pick(line, pick):
        n, wide = pick.shape
        lane = lax.broadcasted_iota(jnp.int32, (8, wide), 1)
        slot_of, vector_of = lane // nv, lane % nv

        def step(k, carry):
            return jnp.where(slot_of == k, vector_of + nv * slot_s[line, k], carry)

        wanted = lax.fori_loop(0, slots, step, jnp.full((8, wide), -1, jnp.int32))[0:1]
        part = CAP * nv

        def fill(i, carry):
            at = lax.broadcasted_iota(jnp.int32, (part, wide), 0) + i * part
            pick[pl.ds(pl.multiple_of(i * part, part), part), :] = jnp.where(
                at == wanted, 1.0, 0.0
            ).astype(BF16)
            return carry

        lax.fori_loop(0, n // part, fill, 0)

    build_pick(0, pick_r)
    build_pick(1, pick_c)
    for c in vec_copies:
        c.wait()
    idx_c.wait_recv()
    idx_r.wait_recv()
    to_smem = pltpu.make_async_copy(idx_v, idx_s, idx_sem)
    to_smem.start()
    to_smem.wait()

    def needed(i, seg_of, j):
        return lax.shift_right_logical(idx_s[i, 0, seg_of * segb + j], 3)

    def position(i, seg_of, b):
        return idx_s[i, 0, seg_of * segb + b] & (NEED - 1)

    def split_blocks(n, source, target):
        def step(i, carry):
            for j in range(CAP):
                high, low = split(source[i, j])
                target[i * CAP + j, 0:nv] = high
                target[i * CAP + j, nv:2 * nv] = low
            return carry

        lax.fori_loop(0, n, step, 0)

    def multiply(line, blocks, pick, n, out, dot, fresh):
        width = chunk

        def step(g, carry):
            for u in range(width):
                k = g * width + u
                x = blocks[jnp.maximum(slot_s[line, k], 0)]
                if fresh:
                    t_hi, t_lo = split(raw[k])
                    tile_hi[k] = t_hi
                    tile_lo[k] = t_lo
                else:
                    t_hi, t_lo = tile_hi[k], tile_lo[k]
                wide = dot(x, t_hi)
                z = wide[0:nv] + wide[nv:2 * nv] + dot(x[0:nv], t_lo)
                high, low = split(z)
                z_hi[k] = high
                z_lo[k] = low
            return carry

        per = chunk // width
        if fresh:
            for i in range(n_chunks):
                tile_copies[i].wait()
                lax.fori_loop(i * per, (i + 1) * per, step, 0)
        else:
            lax.fori_loop(0, n_chunks * per, step, 0)
        flat = (slots * nv, TILE)
        y = dot_nn(pick[...], z_hi[...].reshape(flat)) + dot_nn(pick[...], z_lo[...].reshape(flat))
        out[...] = y.reshape(n, CAP, nv, TILE)

    exchanges = [idx_r, idx_c]

    def apply(which, first, before_rows, after_rows, after_gather, after_columns):
        send_r, send_c, got_r, got_c, back_r, back_c, y_r, y_c = rounds[which][:8]
        gr_s, gc_s, br_s, bc_s, rr = rounds[which][8:]
        gather_r = Exchange("col", lambda p: send_r.at[p], lambda i: got_r.at[i], gr_s, rr.at[0])
        gather_c = Exchange("row", lambda p: send_c.at[p], lambda i: got_c.at[i], gc_s, rr.at[1])
        scatter_r = Exchange("col", lambda p: y_r.at[p], lambda i: back_r.at[i, pl.ds(0, CAP)], br_s, rr.at[2])
        scatter_c = Exchange("row", lambda p: y_c.at[p], lambda i: back_c.at[i, pl.ds(0, CAP)], bc_s, rr.at[3])
        exchanges.extend([gather_r, gather_c, scatter_r, scatter_c])

        def pack(axis, base, exchange, send, got):
            n, me, device = axes[axis]

            def one(p):
                for j in range(CAP):
                    send[p, j] = own[which, needed(base + p, me, j)]
                exchange.make(p, me).start()

            each_peer(axis, one)
            for j in range(CAP):
                got[me, j] = own[which, needed(base + me, me, j)]

        pack("row", n_col, gather_c, send_c, got_c)
        pack("col", 0, gather_r, send_r, got_r)
        first()
        gather_c.wait_recv()
        before_rows()
        split_blocks(n_row, got_c, zc)
        multiply(1, zc, pick_r, n_col, y_r, dot_nt, which == 0)
        scatter_r.start()
        for j in range(CAP):
            back_r[col, j] = y_r[col, j]
        after_rows()
        gather_r.wait_recv()
        split_blocks(n_col, got_r, zr)
        after_gather(y_r)
        multiply(0, zr, pick_c, n_row, y_c, dot_nn, False)
        scatter_c.start()
        for j in range(CAP):
            back_c[row, j] = y_c[row, j]
        after_columns()
        scatter_c.wait_recv()
        scatter_r.wait_recv()
        for b in range(segb):
            total = zero_block
            for i in range(n_row):
                total = total + back_c[i, position(n_col + i, row, b)]
            for i in range(n_col):
                total = total + back_r[i, position(i, col, b)]
            own[which + 1, b] = total

    def own_correlation():
        total = jnp.zeros((nv, nv), F32)
        for b in range(segb):
            total = total + dot_nt(own[0, b], own[0, b], EXACT)
        small[0] = jnp.zeros_like(small[0])
        small[0, 0:nv, 0:nv] = total

    nothing = lambda *unused: None
    apply(0, nothing, nothing, own_correlation, nothing, nothing)

    corr_row = Exchange("row", lambda p: corr_1.at[row], lambda i: corr_1.at[i], c1_s, c1_r)
    corr_col = Exchange("col", lambda p: corr_2.at[col], lambda i: corr_2.at[i], c2_s, c2_r)
    gram_row = Exchange("row", lambda p: gram_1.at[row], lambda i: gram_1.at[i], g1_s, g1_r)
    gram_col = Exchange("col", lambda p: gram_2.at[col], lambda i: gram_2.at[i], g2_s, g2_r)
    exchanges.extend([corr_row, corr_col, gram_row, gram_col])

    def total_of(ref, n):
        total = ref[0]
        for i in range(1, n):
            total = total + ref[i]
        return total

    def fold(total, n):
        return total[0:n, 0:n] + total[0:n, n:2 * n] + total[n:2 * n, 0:n] + total[n:2 * n, n:2 * n]

    def correlate():
        total = jnp.zeros((4 * nv, 4 * nv), F32)
        for b in range(segb):
            both = jnp.concatenate(split(jnp.concatenate([own[0, b], own[1, b]], axis=0)), axis=0)
            total = total + dot_nt(both, both)
        total = fold(total, 2 * nv)
        head = (iota((2 * nv, 2 * nv), 0) < nv) & (iota((2 * nv, 2 * nv), 1) < nv)
        corr_1[row] = pack_square(jnp.where(head, small[0, :, 0:2 * nv], total))
        corr_row.start()

    def correlate_on():
        corr_row.wait_recv()
        corr_2[col] = total_of(corr_1, n_row)
        corr_col.start()

    eye = jnp.where(
        lax.broadcasted_iota(jnp.int32, (nv, nv), 0) == lax.broadcasted_iota(jnp.int32, (nv, nv), 1),
        1.0, 0.0,
    ).astype(F32)

    def gram_terms(y_r):
        def step(i, total):
            for j in range(CAP):
                y = jnp.concatenate(split(y_r[i, j]), axis=0)
                total = total + dot_nt(zr[i * CAP + j], y)
            return total

        total = lax.fori_loop(0, n_col, step, jnp.zeros((2 * nv, 2 * nv), F32))
        half = fold(total, nv)
        gram_1[row] = pack_square(half + dot_nt(eye, half, EXACT))
        gram_row.start()

    def solve():
        gram_row.wait_recv()
        gram_2[col] = total_of(gram_1, n_row)
        gram_col.start()
        corr_col.wait_recv()
        sums = unpack_square(total_of(corr_2, n_col), 2 * nv)
        lanes = 2 * nv
        m = sums[0:nv]
        line = lax.broadcasted_iota(jnp.int32, (nv, lanes), 0)
        lane = lax.broadcasted_iota(jnp.int32, (nv, lanes), 1)
        for i in range(nv):
            pivot_row = m[i:i + 1, :] / m[i:i + 1, i:i + 1]
            m = jnp.where(line == i, pivot_row, m - m[:, i:i + 1] * pivot_row)
        second = jnp.where(lane == line + nv, 1.0, 0.0).astype(F32)
        coeffs_t = dot_nt(second, m, EXACT)
        proj = dot_nt(sums[0:nv], second, EXACT)
        squares = dot_nt(sums[nv:2 * nv], second, EXACT)
        for b in range(segb):
            out_v[:, b * TILE:(b + 1) * TILE] = own[1, b] - dot_nn(coeffs_t, own[0, b], EXACT)
        out_copy.start()
        for b in range(segb):
            later[b] = dot_nn(coeffs_t, own[1, b], EXACT)
        rest = dot_nt(dot_nn(coeffs_t, proj, EXACT), coeffs_t, EXACT)
        rest = rest - dot_nn(coeffs_t, squares, EXACT) - dot_nt(squares, coeffs_t, EXACT)
        small[1, 0:nv, 0:nv] = rest

    out_copy = pltpu.make_async_copy(out_v, residual, out_sem)
    apply(1, correlate, correlate_on, nothing, gram_terms, solve)
    for b in range(segb):
        image[:, b * TILE:(b + 1) * TILE] = own[2, b] - later[b]
    gram_col.wait_recv()
    gram[...] = (unpack_square(total_of(gram_2, n_col), nv) + small[1, 0:nv, 0:nv]) / order
    out_copy.wait()
    for e in exchanges:
        e.wait_send()


def per_device(n_row, n_col, vectors, tiles, tile_rows, tile_cols, counts):
    nv, width = vectors.shape
    segb = width // TILE
    slots = tiles.shape[2]
    smem = pl.BlockSpec(memory_space=pltpu.SMEM)
    vmem = pl.BlockSpec(memory_space=pltpu.VMEM)
    anywhere = pl.BlockSpec(memory_space=pl.ANY)
    hbm = pl.BlockSpec(memory_space=pltpu.HBM)
    in_hbm = lambda x: pltpu.with_memory_space_constraint(x, pltpu.HBM)
    dma = pltpu.SemaphoreType.DMA
    rb, cb = (n_col, CAP, nv, TILE), (n_row, CAP, nv, TILE)
    most = max(n_row, n_col)
    one_round = [
        pltpu.VMEM(rb, F32), pltpu.VMEM(cb, F32), pltpu.VMEM(rb, F32), pltpu.VMEM(cb, F32),
        pltpu.VMEM((n_col, CAP + 1, nv, TILE), F32), pltpu.VMEM((n_row, CAP + 1, nv, TILE), F32),
        pltpu.VMEM(rb, F32), pltpu.VMEM(cb, F32),
        dma((n_col,)), dma((n_row,)), dma((n_col,)), dma((n_row,)), dma((4, most)),
    ]
    scratch = [
        pltpu.VMEM((slots, TILE, TILE), F32),
        pltpu.VMEM((slots, TILE, TILE), BF16),
        pltpu.VMEM((slots, TILE, TILE), BF16),
        pltpu.VMEM((n_col * CAP * nv, slots * nv), BF16),
        pltpu.VMEM((n_row * CAP * nv, slots * nv), BF16),
        pltpu.VMEM((slots, nv, TILE), BF16),
        pltpu.VMEM((slots, nv, TILE), BF16),
        pltpu.VMEM((n_row + n_col, 1, 128), jnp.int32),
        pltpu.SMEM((n_row + n_col, 1, 128), jnp.int32),
        pltpu.VMEM((3, segb, nv, TILE), F32),
        pltpu.VMEM((n_col * CAP, 2 * nv, TILE), BF16),
        pltpu.VMEM((n_row * CAP, 2 * nv, TILE), BF16),
        pltpu.VMEM((n_row, 4 * nv * nv // 128, 128), F32),
        pltpu.VMEM((n_col, 4 * nv * nv // 128, 128), F32),
        pltpu.VMEM((n_row, nv * nv // 128, 128), F32),
        pltpu.VMEM((n_col, nv * nv // 128, 128), F32),
        pltpu.VMEM((4, 1, 128), jnp.int32),
        pltpu.SMEM((4, 1, 128), jnp.int32),
        pltpu.SMEM((2, slots), jnp.int32),
        pltpu.VMEM((nv, width), F32),
        pltpu.VMEM((segb, nv, TILE), F32),
        pltpu.VMEM((2, 2 * nv, 128), F32),
        dma((slots,)),
        dma(()),
        dma(()),
        dma((segb,)),
        dma(()),
        pltpu.SMEM((1, 1, slots), jnp.int32),
        pltpu.SMEM((1, 1, slots), jnp.int32),
        dma((2,)),
        *one_round,
        *one_round,
        dma((n_col,)), dma((n_col,)), dma((n_row,)), dma((n_row,)),
        dma((n_row,)), dma((n_row,)), dma((n_col,)), dma((n_col,)),
        dma((n_row,)), dma((n_row,)), dma((n_col,)), dma((n_col,)),
    ]
    order = width * n_row * n_col
    return pl.pallas_call(
        functools.partial(main_kernel, n_row, n_col, segb, order),
        out_shape=(
            jax.ShapeDtypeStruct((nv, width), F32),
            jax.ShapeDtypeStruct((nv, width), F32),
            jax.ShapeDtypeStruct((nv, nv), F32),
        ),
        in_specs=[hbm, hbm, smem, hbm, hbm],
        out_specs=(anywhere, vmem, vmem),
        scratch_shapes=scratch,
        compiler_params=pltpu.CompilerParams(
            collective_id=0, has_side_effects=True, vmem_limit_bytes=52 * 2**20
        ),
    )(in_hbm(tile_rows), in_hbm(tile_cols), counts, in_hbm(vectors), tiles)


def solution(mesh):
    in_specs = (
        P(None, ("row", "col")),
        P("row", "col", None, None, None),
        P("row", "col", None),
        P("row", "col", None),
        P("row", "col"),
    )
    out_specs = (P(None, ("row", "col")), P(None, ("row", "col")), P())
    body = functools.partial(per_device, mesh.shape["row"], mesh.shape["col"])
    return jax.shard_map(body, mesh=mesh, in_specs=in_specs, out_specs=out_specs, check_vma=False)
```

```python
import functools

import jax
import jax.numpy as jnp
from jax import lax
from jax.experimental import pallas as pl
from jax.experimental.pallas import tpu as pltpu
from jax.sharding import PartitionSpec as P

TILE = 256
CAP = 3
NEED = 8
MESH = pl.DeviceIdType.MESH
F32 = jnp.float32
BF16 = jnp.bfloat16
EXACT = lax.Precision.HIGHEST


def dot_nt(a, b, precision=None):
    return lax.dot_general(
        a, b, (((1,), (1,)), ((), ())), precision=precision, preferred_element_type=F32
    )


def dot_nn(a, b, precision=None):
    return lax.dot_general(
        a, b, (((1,), (0,)), ((), ())), precision=precision, preferred_element_type=F32
    )


def split(x):
    high = x.astype(BF16)
    return high, (x - high.astype(F32)).astype(BF16)


def iota(shape, dim):
    return lax.broadcasted_iota(jnp.int32, shape, dim)


def one_hot(condition):
    return jnp.where(condition, 1.0, 0.0).astype(F32)


def spread(n):
    per = 128 // n
    lanes = one_hot(iota((n, 128), 1) % n == iota((n, 128), 0))
    kept = one_hot(iota((n, 128), 1) // n == iota((n, 128), 0) % per)
    lines = one_hot(iota((n // per, n), 1) // per == iota((n // per, n), 0))
    back = one_hot(iota((n, n // per), 0) // per == iota((n, n // per), 1))
    return lanes, kept, lines, back


def pack_square(x):
    lanes, kept, lines, _ = spread(x.shape[0])
    return dot_nn(lines, dot_nn(x, lanes, EXACT) * kept, EXACT)


def unpack_square(x, n):
    lanes, kept, _, back = spread(n)
    return dot_nt(dot_nn(back, x, EXACT) * kept, lanes, EXACT)


def main_kernel(n_row, n_col, segb, order, *refs):
    (rows_hbm, cols_hbm, count, vec, tiles, residual, image, gram) = refs[:8]
    refs = refs[8:]
    (
        raw, tile_hi, tile_lo, pick_r, pick_c, z_hi, z_lo, idx_v, idx_s, own,
        zr, zc, corr_1, corr_2, gram_1, gram_2, tab_v, tab_s, slot_s, out_v, later, small,
        tile_sem, idx_sem, tab_sem, vec_sem, out_sem, rows, cols, list_sem,
    ) = refs[:30]
    rounds = [refs[30:45], refs[45:60]]
    (ir_s, ir_r, ic_s, ic_r, c1_s, c1_r, c2_s, c2_r, g1_s, g1_r, g2_s, g2_r) = refs[60:72]
    nv = vec.shape[0]
    slots = raw.shape[0]
    row = lax.axis_index("row")
    col = lax.axis_index("col")
    axes = {
        "row": (n_row, row, lambda p: (p, col)),
        "col": (n_col, col, lambda p: (row, p)),
    }

    def each_peer(axis, body):
        n, me, device = axes[axis]

        def step(d, carry):
            if n & (n - 1):
                body(lax.rem(me + d, n))
            else:
                peer, bit = me, 1
                while bit < n:
                    peer = peer + ((n - d) // bit % 2) * (1 - 2 * (me // bit % 2)) * bit
                    bit *= 2
                body(peer)
            return carry

        lax.fori_loop(1, n, step, 0)

    def copy(axis, source, target, send, recv, p, slot):
        return pltpu.make_async_remote_copy(
            src_ref=source, dst_ref=target, send_sem=send.at[p], recv_sem=recv.at[slot],
            device_id=axes[axis][2](p), device_id_type=MESH,
        )

    class Exchange:
        def __init__(self, axis, source, target, send, recv):
            self.axis, self.source, self.target = axis, source, target
            self.send, self.recv = send, recv

        def make(self, p, slot):
            return copy(self.axis, self.source(p), self.target(slot), self.send, self.recv, p, slot)

        def start(self):
            me = axes[self.axis][1]
            each_peer(self.axis, lambda p: self.make(p, me).start())

        def wait_recv(self):
            each_peer(self.axis, lambda p: self.make(p, p).wait_recv())

        def wait_send(self):
            me = axes[self.axis][1]
            each_peer(self.axis, lambda p: self.make(p, me).wait_send())

    chunk = 8 if slots % 8 == 0 else 1
    n_chunks = slots // chunk
    tile_copies = [
        pltpu.make_async_copy(
            tiles.at[0, 0, pl.ds(i * chunk, chunk)], raw.at[pl.ds(i * chunk, chunk)], tile_sem.at[i]
        )
        for i in range(n_chunks)
    ]
    vec_copies = [
        pltpu.make_async_copy(vec.at[:, pl.ds(b * TILE, TILE)], own.at[0, b], vec_sem.at[b])
        for b in range(segb)
    ]
    list_copies = [
        pltpu.make_async_copy(rows_hbm, rows, list_sem.at[0]),
        pltpu.make_async_copy(cols_hbm, cols, list_sem.at[1]),
    ]
    for c in list_copies + vec_copies + tile_copies:
        c.start()

    barrier = pltpu.get_barrier_semaphore()
    for axis in ("row", "col"):
        device = axes[axis][2]
        each_peer(
            axis,
            lambda p: pl.semaphore_signal(
                barrier, inc=1, device_id=device(p), device_id_type=MESH
            ),
        )

    lane = lax.broadcasted_iota(jnp.int32, (8, 128), 1)
    line = lax.broadcasted_iota(jnp.int32, (8, 128), 0)
    live_count = count[0, 0]
    seg = jnp.zeros((8, 128), jnp.int32)
    for i in range(1, 128 // segb + 1):
        seg = seg + (lane >= i * segb).astype(jnp.int32)
    block = lane - seg * segb

    def touch(g, named):
        for u in range(unroll):
            k = g * unroll + u
            live = k < live_count
            which = jnp.where(
                line == 0, jnp.where(live, rows[0, 0, k], -1), jnp.where(live, cols[0, 0, k], -1)
            )
            named = jnp.where(lane == which, 1, named)
        return named

    unroll = 8 if slots % 8 == 0 else 1
    for c in list_copies:
        c.wait()
    named = lax.fori_loop(0, slots // unroll, touch, jnp.zeros((8, 128), jnp.int32))
    rank = jnp.zeros((8, 128), jnp.int32)
    for d in range(1, segb):
        rank = rank + jnp.where(block >= d, pltpu.roll(named, d, 1), 0)
    need = jnp.zeros((8, 128), jnp.int32)
    for d in range(segb):
        moved = jnp.where((named > 0) & (block - rank == d), block, 0)
        need = need + (pltpu.roll(moved, 128 - d, 1) if d else moved)
    message = jnp.where(named > 0, rank, CAP) + NEED * need
    place = seg * CAP + rank
    tab_v[0] = message[0:1]
    tab_v[1] = message[1:2]
    tab_v[2] = place[0:1]
    tab_v[3] = place[1:2]
    idx_v[col] = message[0:1]
    idx_v[n_col + row] = message[1:2]
    to_tab = pltpu.make_async_copy(tab_v, tab_s, tab_sem)
    to_tab.start()
    part_nv = nv // 2
    zero_block = jnp.zeros((part_nv, TILE), F32)
    for r in rounds:
        for h in range(2):
            for i in range(n_col):
                r[4 + h][i, CAP] = zero_block
            for i in range(n_row):
                r[6 + h][i, CAP] = zero_block
    pl.semaphore_wait(barrier, n_row + n_col - 2)

    idx_r = Exchange("col", lambda p: tab_v.at[0], lambda i: idx_v.at[i], ir_s, ir_r)
    idx_c = Exchange("row", lambda p: tab_v.at[1], lambda i: idx_v.at[n_col + i], ic_s, ic_r)
    idx_r.start()
    idx_c.start()
    to_tab.wait()

    def place_slots(k, carry):
        live = k < live_count
        slot_s[0, k] = jnp.where(live, tab_s[2, 0, rows[0, 0, k]], -1)
        slot_s[1, k] = jnp.where(live, tab_s[3, 0, cols[0, 0, k]], -1)
        return carry

    lax.fori_loop(0, slots, place_slots, 0)

    def build_pick(line, pick):
        n, wide = pick.shape
        lane = lax.broadcasted_iota(jnp.int32, (8, wide), 1)
        slot_of, vector_of = lane // nv, lane % nv

        def step(k, carry):
            return jnp.where(slot_of == k, vector_of + nv * slot_s[line, k], carry)

        wanted = lax.fori_loop(0, slots, step, jnp.full((8, wide), -1, jnp.int32))[0:1]
        part = CAP * nv

        def fill(i, carry):
            at = lax.broadcasted_iota(jnp.int32, (part, wide), 0) + i * part
            pick[pl.ds(pl.multiple_of(i * part, part), part), :] = jnp.where(
                at == wanted, 1.0, 0.0
            ).astype(BF16)
            return carry

        lax.fori_loop(0, n // part, fill, 0)

    build_pick(0, pick_r)
    build_pick(1, pick_c)
    for c in vec_copies:
        c.wait()
    idx_c.wait_recv()
    idx_r.wait_recv()
    to_smem = pltpu.make_async_copy(idx_v, idx_s, idx_sem)
    to_smem.start()
    to_smem.wait()

    def needed(i, seg_of, j):
        return lax.shift_right_logical(idx_s[i, 0, seg_of * segb + j], 3)

    def position(i, seg_of, b):
        return idx_s[i, 0, seg_of * segb + b] & (NEED - 1)

    def split_blocks(n, source, target):
        def step(i, carry):
            for j in range(CAP):
                high, low = split(source[i, j])
                target[i * CAP + j, 0:nv] = high
                target[i * CAP + j, nv:2 * nv] = low
            return carry

        lax.fori_loop(0, n, step, 0)

    def multiply(line, blocks, pick, n, out, dot, fresh):
        width = chunk

        def step(g, carry):
            for u in range(width):
                k = g * width + u
                x = blocks[jnp.maximum(slot_s[line, k], 0)]
                if fresh:
                    t_hi, t_lo = split(raw[k])
                    tile_hi[k] = t_hi
                    tile_lo[k] = t_lo
                else:
                    t_hi, t_lo = tile_hi[k], tile_lo[k]
                wide = dot(x, t_hi)
                z = wide[0:nv] + wide[nv:2 * nv] + dot(x[0:nv], t_lo)
                high, low = split(z)
                z_hi[k] = high
                z_lo[k] = low
            return carry

        per = chunk // width
        if fresh:
            for i in range(n_chunks):
                tile_copies[i].wait()
                lax.fori_loop(i * per, (i + 1) * per, step, 0)
        else:
            lax.fori_loop(0, n_chunks * per, step, 0)
        flat = (slots * nv, TILE)
        y = dot_nn(pick[...], z_hi[...].reshape(flat)) + dot_nn(pick[...], z_lo[...].reshape(flat))
        out[...] = y.reshape(n, CAP, nv, TILE)

    exchanges = [idx_r, idx_c]

    class Round:
        def __init__(self, which):
            self.which = which
            send_r, send_c, got_r, got_c, ra, rb, ca, cb, y_r, y_c = rounds[which][:10]
            gr_s, gc_s, br_s, bc_s, arrived = rounds[which][10:]
            self.send_r, self.send_c, self.got_r, self.got_c = send_r, send_c, got_r, got_c
            self.back_r, self.back_c, self.y_r, self.y_c = (ra, rb), (ca, cb), y_r, y_c

            def half(axis, source, target, send, h, at):
                e = Exchange(axis, source, target, send.at[h], arrived.at[2 * at + h])
                exchanges.append(e)
                return e

            def of(h):
                return pl.ds(h * part_nv, part_nv)

            both = range(2)
            self.gather_r = [half("col", lambda p, h=h: send_r.at[p, :, of(h)], lambda i, h=h: got_r.at[i, :, of(h)], gr_s, h, 0) for h in both]
            self.gather_c = [half("row", lambda p, h=h: send_c.at[p, :, of(h)], lambda i, h=h: got_c.at[i, :, of(h)], gc_s, h, 1) for h in both]
            self.scatter_r = [half("col", lambda p, h=h: y_r.at[p, :, of(h)], lambda i, h=h: self.back_r[h].at[i, pl.ds(0, CAP)], br_s, h, 2) for h in both]
            self.scatter_c = [half("row", lambda p, h=h: y_c.at[p, :, of(h)], lambda i, h=h: self.back_c[h].at[i, pl.ds(0, CAP)], bc_s, h, 3) for h in both]

        def pack(self, h):
            rows_of = slice(h * part_nv, (h + 1) * part_nv)
            for axis, base, exchange, send, got in (
                ("row", n_col, self.gather_c[h], self.send_c, self.got_c),
                ("col", 0, self.gather_r[h], self.send_r, self.got_r),
            ):
                me = axes[axis][1]

                def one(p):
                    for j in range(CAP):
                        send[p, j, rows_of] = own[self.which, needed(base + p, me, j), rows_of]
                    exchange.make(p, me).start()

                each_peer(axis, one)
                for j in range(CAP):
                    got[me, j, rows_of] = own[self.which, needed(base + me, me, j), rows_of]

        def scatter(self, exchange, back, y, me):
            for h in range(2):
                exchange[h].start()
            for h in range(2):
                for j in range(CAP):
                    back[h][me, j] = y[me, j, h * part_nv:(h + 1) * part_nv]

        def apply(self, first, before_rows, after_rows, after_gather, after_columns, after_half):
            first()
            for h in range(2):
                self.gather_c[h].wait_recv()
            before_rows()
            split_blocks(n_row, self.got_c, zc)
            multiply(1, zc, pick_r, n_col, self.y_r, dot_nt, self.which == 0)
            self.scatter(self.scatter_r, self.back_r, self.y_r, col)
            after_rows()
            for h in range(2):
                self.gather_r[h].wait_recv()
            split_blocks(n_col, self.got_r, zr)
            after_gather(self.y_r)
            multiply(0, zr, pick_c, n_row, self.y_c, dot_nn, False)
            self.scatter(self.scatter_c, self.back_c, self.y_c, row)
            after_columns()
            for h in range(2):
                self.scatter_c[h].wait_recv()
                self.scatter_r[h].wait_recv()
                for b in range(segb):
                    total = zero_block
                    for i in range(n_row):
                        total = total + self.back_c[h][i, position(n_col + i, row, b)]
                    for i in range(n_col):
                        total = total + self.back_r[h][i, position(i, col, b)]
                    own[self.which + 1, b, h * part_nv:(h + 1) * part_nv] = total
                after_half(h)

    def own_correlation():
        total = jnp.zeros((nv, nv), F32)
        for b in range(segb):
            total = total + dot_nt(own[0, b], own[0, b], EXACT)
        small[0] = jnp.zeros_like(small[0])
        small[0, 0:nv, 0:nv] = total

    nothing = lambda *unused: None
    one, two = Round(0), Round(1)
    for h in range(2):
        one.pack(h)
    one.apply(nothing, nothing, own_correlation, nothing, nothing, two.pack)

    corr_row = Exchange("row", lambda p: corr_1.at[row], lambda i: corr_1.at[i], c1_s, c1_r)
    corr_col = Exchange("col", lambda p: corr_2.at[col], lambda i: corr_2.at[i], c2_s, c2_r)
    gram_row = Exchange("row", lambda p: gram_1.at[row], lambda i: gram_1.at[i], g1_s, g1_r)
    gram_col = Exchange("col", lambda p: gram_2.at[col], lambda i: gram_2.at[i], g2_s, g2_r)
    exchanges.extend([corr_row, corr_col, gram_row, gram_col])

    def total_of(ref, n):
        total = ref[0]
        for i in range(1, n):
            total = total + ref[i]
        return total

    def fold(total, n):
        return total[0:n, 0:n] + total[0:n, n:2 * n] + total[n:2 * n, 0:n] + total[n:2 * n, n:2 * n]

    def correlate():
        total = jnp.zeros((4 * nv, 4 * nv), F32)
        for b in range(segb):
            both = jnp.concatenate(split(jnp.concatenate([own[0, b], own[1, b]], axis=0)), axis=0)
            total = total + dot_nt(both, both)
        total = fold(total, 2 * nv)
        head = (iota((2 * nv, 2 * nv), 0) < nv) & (iota((2 * nv, 2 * nv), 1) < nv)
        corr_1[row] = pack_square(jnp.where(head, small[0, :, 0:2 * nv], total))
        corr_row.start()

    def correlate_on():
        corr_row.wait_recv()
        corr_2[col] = total_of(corr_1, n_row)
        corr_col.start()

    eye = jnp.where(
        lax.broadcasted_iota(jnp.int32, (nv, nv), 0) == lax.broadcasted_iota(jnp.int32, (nv, nv), 1),
        1.0, 0.0,
    ).astype(F32)

    def gram_terms(y_r):
        def step(i, total):
            for j in range(CAP):
                y = jnp.concatenate(split(y_r[i, j]), axis=0)
                total = total + dot_nt(zr[i * CAP + j], y)
            return total

        total = lax.fori_loop(0, n_col, step, jnp.zeros((2 * nv, 2 * nv), F32))
        half = fold(total, nv)
        gram_1[row] = pack_square(half + dot_nt(eye, half, EXACT))
        gram_row.start()

    def solve():
        gram_row.wait_recv()
        gram_2[col] = total_of(gram_1, n_row)
        gram_col.start()
        corr_col.wait_recv()
        sums = unpack_square(total_of(corr_2, n_col), 2 * nv)
        lanes = 2 * nv
        m = sums[0:nv]
        line = lax.broadcasted_iota(jnp.int32, (nv, lanes), 0)
        lane = lax.broadcasted_iota(jnp.int32, (nv, lanes), 1)
        for i in range(nv):
            pivot_row = m[i:i + 1, :] / m[i:i + 1, i:i + 1]
            m = jnp.where(line == i, pivot_row, m - m[:, i:i + 1] * pivot_row)
        second = jnp.where(lane == line + nv, 1.0, 0.0).astype(F32)
        coeffs_t = dot_nt(second, m, EXACT)
        proj = dot_nt(sums[0:nv], second, EXACT)
        squares = dot_nt(sums[nv:2 * nv], second, EXACT)
        for b in range(segb):
            out_v[:, b * TILE:(b + 1) * TILE] = own[1, b] - dot_nn(coeffs_t, own[0, b], EXACT)
        out_copy.start()
        for b in range(segb):
            later[b] = dot_nn(coeffs_t, own[1, b], EXACT)
        rest = dot_nt(dot_nn(coeffs_t, proj, EXACT), coeffs_t, EXACT)
        rest = rest - dot_nn(coeffs_t, squares, EXACT) - dot_nt(squares, coeffs_t, EXACT)
        small[1, 0:nv, 0:nv] = rest

    out_copy = pltpu.make_async_copy(out_v, residual, out_sem)
    two.apply(correlate, correlate_on, nothing, gram_terms, solve, nothing)
    for b in range(segb):
        image[:, b * TILE:(b + 1) * TILE] = own[2, b] - later[b]
    gram_col.wait_recv()
    gram[...] = (unpack_square(total_of(gram_2, n_col), nv) + small[1, 0:nv, 0:nv]) / order
    out_copy.wait()
    for e in exchanges:
        e.wait_send()


def per_device(n_row, n_col, vectors, tiles, tile_rows, tile_cols, counts):
    nv, width = vectors.shape
    segb = width // TILE
    slots = tiles.shape[2]
    smem = pl.BlockSpec(memory_space=pltpu.SMEM)
    vmem = pl.BlockSpec(memory_space=pltpu.VMEM)
    anywhere = pl.BlockSpec(memory_space=pl.ANY)
    hbm = pl.BlockSpec(memory_space=pltpu.HBM)
    in_hbm = lambda x: pltpu.with_memory_space_constraint(x, pltpu.HBM)
    dma = pltpu.SemaphoreType.DMA
    rb, cb = (n_col, CAP, nv, TILE), (n_row, CAP, nv, TILE)
    most = max(n_row, n_col)
    one_round = [
        pltpu.VMEM(rb, F32), pltpu.VMEM(cb, F32), pltpu.VMEM(rb, F32), pltpu.VMEM(cb, F32),
        *[pltpu.VMEM((n_col, CAP + 1, nv // 2, TILE), F32)] * 2,
        *[pltpu.VMEM((n_row, CAP + 1, nv // 2, TILE), F32)] * 2,
        pltpu.VMEM(rb, F32), pltpu.VMEM(cb, F32),
        dma((2, n_col)), dma((2, n_row)), dma((2, n_col)), dma((2, n_row)), dma((8, most)),
    ]
    scratch = [
        pltpu.VMEM((slots, TILE, TILE), F32),
        pltpu.VMEM((slots, TILE, TILE), BF16),
        pltpu.VMEM((slots, TILE, TILE), BF16),
        pltpu.VMEM((n_col * CAP * nv, slots * nv), BF16),
        pltpu.VMEM((n_row * CAP * nv, slots * nv), BF16),
        pltpu.VMEM((slots, nv, TILE), BF16),
        pltpu.VMEM((slots, nv, TILE), BF16),
        pltpu.VMEM((n_row + n_col, 1, 128), jnp.int32),
        pltpu.SMEM((n_row + n_col, 1, 128), jnp.int32),
        pltpu.VMEM((3, segb, nv, TILE), F32),
        pltpu.VMEM((n_col * CAP, 2 * nv, TILE), BF16),
        pltpu.VMEM((n_row * CAP, 2 * nv, TILE), BF16),
        pltpu.VMEM((n_row, 4 * nv * nv // 128, 128), F32),
        pltpu.VMEM((n_col, 4 * nv * nv // 128, 128), F32),
        pltpu.VMEM((n_row, nv * nv // 128, 128), F32),
        pltpu.VMEM((n_col, nv * nv // 128, 128), F32),
        pltpu.VMEM((4, 1, 128), jnp.int32),
        pltpu.SMEM((4, 1, 128), jnp.int32),
        pltpu.SMEM((2, slots), jnp.int32),
        pltpu.VMEM((nv, width), F32),
        pltpu.VMEM((segb, nv, TILE), F32),
        pltpu.VMEM((2, 2 * nv, 128), F32),
        dma((slots,)),
        dma(()),
        dma(()),
        dma((segb,)),
        dma(()),
        pltpu.SMEM((1, 1, slots), jnp.int32),
        pltpu.SMEM((1, 1, slots), jnp.int32),
        dma((2,)),
        *one_round,
        *one_round,
        dma((n_col,)), dma((n_col,)), dma((n_row,)), dma((n_row,)),
        dma((n_row,)), dma((n_row,)), dma((n_col,)), dma((n_col,)),
        dma((n_row,)), dma((n_row,)), dma((n_col,)), dma((n_col,)),
    ]
    order = width * n_row * n_col
    return pl.pallas_call(
        functools.partial(main_kernel, n_row, n_col, segb, order),
        out_shape=(
            jax.ShapeDtypeStruct((nv, width), F32),
            jax.ShapeDtypeStruct((nv, width), F32),
            jax.ShapeDtypeStruct((nv, nv), F32),
        ),
        in_specs=[hbm, hbm, smem, hbm, hbm],
        out_specs=(anywhere, vmem, vmem),
        scratch_shapes=scratch,
        compiler_params=pltpu.CompilerParams(
            collective_id=0, has_side_effects=True, vmem_limit_bytes=52 * 2**20
        ),
    )(in_hbm(tile_rows), in_hbm(tile_cols), counts, in_hbm(vectors), tiles)


def solution(mesh):
    in_specs = (
        P(None, ("row", "col")),
        P("row", "col", None, None, None),
        P("row", "col", None),
        P("row", "col", None),
        P("row", "col"),
    )
    out_specs = (P(None, ("row", "col")), P(None, ("row", "col")), P())
    body = functools.partial(per_device, mesh.shape["row"], mesh.shape["col"])
    return jax.shard_map(body, mesh=mesh, in_specs=in_specs, out_specs=out_specs, check_vma=False)
```

```python
import functools

import jax
import jax.numpy as jnp
from jax import lax
from jax.experimental import pallas as pl
from jax.experimental.pallas import tpu as pltpu
from jax.sharding import PartitionSpec as P

TILE = 256
CAP = 3
NEED = 8
MESH = pl.DeviceIdType.MESH
F32 = jnp.float32
BF16 = jnp.bfloat16
EXACT = lax.Precision.HIGHEST


def dot_nt(a, b, precision=None):
    return lax.dot_general(
        a, b, (((1,), (1,)), ((), ())), precision=precision, preferred_element_type=F32
    )


def dot_nn(a, b, precision=None):
    return lax.dot_general(
        a, b, (((1,), (0,)), ((), ())), precision=precision, preferred_element_type=F32
    )


def split(x):
    high = x.astype(BF16)
    return high, (x - high.astype(F32)).astype(BF16)


def iota(shape, dim):
    return lax.broadcasted_iota(jnp.int32, shape, dim)


def one_hot(condition):
    return jnp.where(condition, 1.0, 0.0).astype(F32)


def spread(n):
    per = 128 // n
    lanes = one_hot(iota((n, 128), 1) % n == iota((n, 128), 0))
    kept = one_hot(iota((n, 128), 1) // n == iota((n, 128), 0) % per)
    lines = one_hot(iota((n // per, n), 1) // per == iota((n // per, n), 0))
    back = one_hot(iota((n, n // per), 0) // per == iota((n, n // per), 1))
    return lanes, kept, lines, back


def pack_square(x):
    lanes, kept, lines, _ = spread(x.shape[0])
    return dot_nn(lines, dot_nn(x, lanes, EXACT) * kept, EXACT)


def unpack_square(x, n):
    lanes, kept, _, back = spread(n)
    return dot_nt(dot_nn(back, x, EXACT) * kept, lanes, EXACT)


def main_kernel(n_row, n_col, segb, order, *refs):
    (rows_hbm, cols_hbm, count, vec, tiles, residual, image, gram) = refs[:8]
    refs = refs[8:]
    (
        raw, tile_hi, tile_lo, pick_r, pick_c, z_hi, z_lo, idx_v, idx_s, own,
        zr, zc, corr_1, corr_2, gram_1, gram_2, tab_v, tab_s, slot_s, out_v, later, small,
        tile_sem, idx_sem, tab_sem, vec_sem, out_sem, rows, cols, list_sem,
    ) = refs[:30]
    rounds = [refs[30:45], refs[45:60]]
    (ir_s, ir_r, ic_s, ic_r, c1_s, c1_r, c2_s, c2_r, g1_s, g1_r, g2_s, g2_r) = refs[60:72]
    nv = vec.shape[0]
    slots = raw.shape[0]
    row = lax.axis_index("row")
    col = lax.axis_index("col")
    axes = {
        "row": (n_row, row, lambda p: (p, col)),
        "col": (n_col, col, lambda p: (row, p)),
    }

    def each_peer(axis, body):
        n, me, device = axes[axis]

        def step(d, carry):
            if n & (n - 1):
                body(lax.rem(me + d, n))
            else:
                peer, bit = me, 1
                while bit < n:
                    peer = peer + ((n - d) // bit % 2) * (1 - 2 * (me // bit % 2)) * bit
                    bit *= 2
                body(peer)
            return carry

        lax.fori_loop(1, n, step, 0)

    def copy(axis, source, target, send, recv, p, slot):
        return pltpu.make_async_remote_copy(
            src_ref=source, dst_ref=target, send_sem=send.at[p], recv_sem=recv.at[slot],
            device_id=axes[axis][2](p), device_id_type=MESH,
        )

    class Exchange:
        def __init__(self, axis, source, target, send, recv):
            self.axis, self.source, self.target = axis, source, target
            self.send, self.recv = send, recv

        def make(self, p, slot):
            return copy(self.axis, self.source(p), self.target(slot), self.send, self.recv, p, slot)

        def start(self):
            me = axes[self.axis][1]
            each_peer(self.axis, lambda p: self.make(p, me).start())

        def wait_recv(self):
            each_peer(self.axis, lambda p: self.make(p, p).wait_recv())

        def wait_send(self):
            me = axes[self.axis][1]
            each_peer(self.axis, lambda p: self.make(p, me).wait_send())

    chunk = 8 if slots % 8 == 0 else 1
    n_chunks = slots // chunk
    tile_copies = [
        pltpu.make_async_copy(
            tiles.at[0, 0, pl.ds(i * chunk, chunk)], raw.at[pl.ds(i * chunk, chunk)], tile_sem.at[i]
        )
        for i in range(n_chunks)
    ]
    vec_copies = [
        pltpu.make_async_copy(vec.at[:, pl.ds(b * TILE, TILE)], own.at[0, b], vec_sem.at[b])
        for b in range(segb)
    ]
    list_copies = [
        pltpu.make_async_copy(rows_hbm, rows, list_sem.at[0]),
        pltpu.make_async_copy(cols_hbm, cols, list_sem.at[1]),
    ]
    for c in list_copies + vec_copies + tile_copies:
        c.start()

    barrier = pltpu.get_barrier_semaphore()
    for axis in ("row", "col"):
        device = axes[axis][2]
        each_peer(
            axis,
            lambda p: pl.semaphore_signal(
                barrier, inc=1, device_id=device(p), device_id_type=MESH
            ),
        )

    lane = lax.broadcasted_iota(jnp.int32, (8, 128), 1)
    line = lax.broadcasted_iota(jnp.int32, (8, 128), 0)
    live_count = count[0, 0]
    seg = jnp.zeros((8, 128), jnp.int32)
    for i in range(1, 128 // segb + 1):
        seg = seg + (lane >= i * segb).astype(jnp.int32)
    block = lane - seg * segb

    def touch(g, named):
        for u in range(unroll):
            k = g * unroll + u
            live = k < live_count
            which = jnp.where(
                line == 0, jnp.where(live, rows[0, 0, k], -1), jnp.where(live, cols[0, 0, k], -1)
            )
            named = jnp.where(lane == which, 1, named)
        return named

    unroll = 8 if slots % 8 == 0 else 1
    for c in list_copies:
        c.wait()
    named = lax.fori_loop(0, slots // unroll, touch, jnp.zeros((8, 128), jnp.int32))
    rank = jnp.zeros((8, 128), jnp.int32)
    for d in range(1, segb):
        rank = rank + jnp.where(block >= d, pltpu.roll(named, d, 1), 0)
    need = jnp.zeros((8, 128), jnp.int32)
    for d in range(segb):
        moved = jnp.where((named > 0) & (block - rank == d), block, 0)
        need = need + (pltpu.roll(moved, 128 - d, 1) if d else moved)
    message = jnp.where(named > 0, rank, CAP) + NEED * need
    place = seg * CAP + rank
    tab_v[0] = message[0:1]
    tab_v[1] = message[1:2]
    tab_v[2] = place[0:1]
    tab_v[3] = place[1:2]
    idx_v[col] = message[0:1]
    idx_v[n_col + row] = message[1:2]
    to_tab = pltpu.make_async_copy(tab_v, tab_s, tab_sem)
    to_tab.start()
    part_nv = nv // 2
    zero_block = jnp.zeros((part_nv, TILE), F32)
    for r in rounds:
        for h in range(2):
            for i in range(n_col):
                r[4 + h][i, CAP] = zero_block
            for i in range(n_row):
                r[6 + h][i, CAP] = zero_block
    pl.semaphore_wait(barrier, n_row + n_col - 2)

    idx_r = Exchange("col", lambda p: tab_v.at[0], lambda i: idx_v.at[i], ir_s, ir_r)
    idx_c = Exchange("row", lambda p: tab_v.at[1], lambda i: idx_v.at[n_col + i], ic_s, ic_r)
    idx_r.start()
    idx_c.start()
    to_tab.wait()

    def place_slots(k, carry):
        live = k < live_count
        slot_s[0, k] = jnp.where(live, tab_s[2, 0, rows[0, 0, k]], -1)
        slot_s[1, k] = jnp.where(live, tab_s[3, 0, cols[0, 0, k]], -1)
        return carry

    lax.fori_loop(0, slots, place_slots, 0)

    def build_pick(line, pick):
        n, wide = pick.shape
        lane = lax.broadcasted_iota(jnp.int32, (8, wide), 1)
        slot_of, vector_of = lane // nv, lane % nv

        def step(k, carry):
            return jnp.where(slot_of == k, vector_of + nv * slot_s[line, k], carry)

        wanted = lax.fori_loop(0, slots, step, jnp.full((8, wide), -1, jnp.int32))[0:1]
        part = CAP * nv

        def fill(i, carry):
            at = lax.broadcasted_iota(jnp.int32, (part, wide), 0) + i * part
            pick[pl.ds(pl.multiple_of(i * part, part), part), :] = jnp.where(
                at == wanted, 1.0, 0.0
            ).astype(BF16)
            return carry

        lax.fori_loop(0, n // part, fill, 0)

    build_pick(0, pick_r)
    build_pick(1, pick_c)
    for c in vec_copies:
        c.wait()
    idx_c.wait_recv()
    idx_r.wait_recv()
    to_smem = pltpu.make_async_copy(idx_v, idx_s, idx_sem)
    to_smem.start()
    to_smem.wait()

    def needed(i, seg_of, j):
        return lax.shift_right_logical(idx_s[i, 0, seg_of * segb + j], 3)

    def position(i, seg_of, b):
        return idx_s[i, 0, seg_of * segb + b] & (NEED - 1)

    def split_blocks(n, source, target):
        def step(i, carry):
            for j in range(CAP):
                high, low = split(source[i, j])
                target[i * CAP + j, 0:nv] = high
                target[i * CAP + j, nv:2 * nv] = low
            return carry

        lax.fori_loop(0, n, step, 0)

    def split_tiles():
        def step(g, carry):
            for u in range(pair):
                high, low = split(raw[g * pair + u])
                tile_hi[g * pair + u] = high
                tile_lo[g * pair + u] = low
            return carry

        pair = 2 if chunk % 2 == 0 else 1
        per = chunk // pair
        for i in range(n_chunks):
            tile_copies[i].wait()
            lax.fori_loop(i * per, (i + 1) * per, step, 0)

    def multiply(line, blocks, pick, n, out, dot):
        width = 16 if slots % 16 == 0 else 1

        def step(g, carry):
            for u in range(width):
                k = g * width + u
                x = blocks[jnp.maximum(slot_s[line, k], 0)]
                wide = dot(x, tile_hi[k])
                z = wide[0:nv] + wide[nv:2 * nv] + dot(x[0:nv], tile_lo[k])
                high, low = split(z)
                z_hi[k] = high
                z_lo[k] = low
            return carry

        lax.fori_loop(0, slots // width, step, 0)
        flat = (slots * nv, TILE)
        y = dot_nn(pick[...], z_hi[...].reshape(flat)) + dot_nn(pick[...], z_lo[...].reshape(flat))
        out[...] = y.reshape(n, CAP, nv, TILE)

    exchanges = [idx_r, idx_c]

    class Round:
        def __init__(self, which):
            self.which = which
            send_r, send_c, got_r, got_c, ra, rb, ca, cb, y_r, y_c = rounds[which][:10]
            gr_s, gc_s, br_s, bc_s, arrived = rounds[which][10:]
            self.send_r, self.send_c, self.got_r, self.got_c = send_r, send_c, got_r, got_c
            self.back_r, self.back_c, self.y_r, self.y_c = (ra, rb), (ca, cb), y_r, y_c

            def half(axis, source, target, send, h, at):
                e = Exchange(axis, source, target, send.at[h], arrived.at[2 * at + h])
                exchanges.append(e)
                return e

            def of(h):
                return pl.ds(h * part_nv, part_nv)

            both = range(2)
            self.gather_r = [half("col", lambda p, h=h: send_r.at[p, :, of(h)], lambda i, h=h: got_r.at[i, :, of(h)], gr_s, h, 0) for h in both]
            self.gather_c = [half("row", lambda p, h=h: send_c.at[p, :, of(h)], lambda i, h=h: got_c.at[i, :, of(h)], gc_s, h, 1) for h in both]
            self.scatter_r = [half("col", lambda p, h=h: y_r.at[p, :, of(h)], lambda i, h=h: self.back_r[h].at[i, pl.ds(0, CAP)], br_s, h, 2) for h in both]
            self.scatter_c = [half("row", lambda p, h=h: y_c.at[p, :, of(h)], lambda i, h=h: self.back_c[h].at[i, pl.ds(0, CAP)], bc_s, h, 3) for h in both]

        def pack(self, h):
            rows_of = slice(h * part_nv, (h + 1) * part_nv)
            for axis, base, exchange, send, got in (
                ("row", n_col, self.gather_c[h], self.send_c, self.got_c),
                ("col", 0, self.gather_r[h], self.send_r, self.got_r),
            ):
                me = axes[axis][1]

                def one(p):
                    for j in range(CAP):
                        send[p, j, rows_of] = own[self.which, needed(base + p, me, j), rows_of]
                    exchange.make(p, me).start()

                each_peer(axis, one)
                for j in range(CAP):
                    got[me, j, rows_of] = own[self.which, needed(base + me, me, j), rows_of]

        def scatter(self, exchange, back, y, me):
            for h in range(2):
                exchange[h].start()
            for h in range(2):
                for j in range(CAP):
                    back[h][me, j] = y[me, j, h * part_nv:(h + 1) * part_nv]

        def apply(self, first, before_scatter, after_rows, after_gather, after_columns, after_half):
            first()
            for h in range(2):
                self.gather_c[h].wait_recv()
            split_blocks(n_row, self.got_c, zc)
            multiply(1, zc, pick_r, n_col, self.y_r, dot_nt)
            before_scatter()
            self.scatter(self.scatter_r, self.back_r, self.y_r, col)
            after_rows()
            for h in range(2):
                self.gather_r[h].wait_recv()
            split_blocks(n_col, self.got_r, zr)
            after_gather(self.y_r)
            multiply(0, zr, pick_c, n_row, self.y_c, dot_nn)
            self.scatter(self.scatter_c, self.back_c, self.y_c, row)
            after_columns()
            for h in range(2):
                self.scatter_c[h].wait_recv()
                self.scatter_r[h].wait_recv()
                for b in range(segb):
                    total = zero_block
                    for i in range(n_row):
                        total = total + self.back_c[h][i, position(n_col + i, row, b)]
                    for i in range(n_col):
                        total = total + self.back_r[h][i, position(i, col, b)]
                    own[self.which + 1, b, h * part_nv:(h + 1) * part_nv] = total
                after_half(h)

    def own_correlation():
        total = jnp.zeros((nv, nv), F32)
        for b in range(segb):
            total = total + dot_nt(own[0, b], own[0, b], EXACT)
        small[0] = jnp.zeros_like(small[0])
        small[0, 0:nv, 0:nv] = total

    nothing = lambda *unused: None
    one, two = Round(0), Round(1)
    for h in range(2):
        one.pack(h)
    one.apply(split_tiles, nothing, own_correlation, nothing, nothing, two.pack)

    corr_row = Exchange("row", lambda p: corr_1.at[row], lambda i: corr_1.at[i], c1_s, c1_r)
    corr_col = Exchange("col", lambda p: corr_2.at[col], lambda i: corr_2.at[i], c2_s, c2_r)
    gram_row = Exchange("row", lambda p: gram_1.at[row], lambda i: gram_1.at[i], g1_s, g1_r)
    gram_col = Exchange("col", lambda p: gram_2.at[col], lambda i: gram_2.at[i], g2_s, g2_r)
    exchanges.extend([corr_row, corr_col, gram_row, gram_col])

    def total_of(ref, n):
        total = ref[0]
        for i in range(1, n):
            total = total + ref[i]
        return total

    def fold(total, n):
        return total[0:n, 0:n] + total[0:n, n:2 * n] + total[n:2 * n, 0:n] + total[n:2 * n, n:2 * n]

    def correlate():
        total = jnp.zeros((4 * nv, 4 * nv), F32)
        for b in range(segb):
            both = jnp.concatenate(split(jnp.concatenate([own[0, b], own[1, b]], axis=0)), axis=0)
            total = total + dot_nt(both, both)
        total = fold(total, 2 * nv)
        head = (iota((2 * nv, 2 * nv), 0) < nv) & (iota((2 * nv, 2 * nv), 1) < nv)
        corr_1[row] = pack_square(jnp.where(head, small[0, :, 0:2 * nv], total))
        corr_row.start()

    def correlate_on():
        corr_row.wait_recv()
        corr_2[col] = total_of(corr_1, n_row)
        corr_col.start()

    eye = jnp.where(
        lax.broadcasted_iota(jnp.int32, (nv, nv), 0) == lax.broadcasted_iota(jnp.int32, (nv, nv), 1),
        1.0, 0.0,
    ).astype(F32)

    def gram_terms(y_r):
        def step(i, total):
            for j in range(CAP):
                y = jnp.concatenate(split(y_r[i, j]), axis=0)
                total = total + dot_nt(zr[i * CAP + j], y)
            return total

        total = lax.fori_loop(0, n_col, step, jnp.zeros((2 * nv, 2 * nv), F32))
        half = fold(total, nv)
        gram_1[row] = pack_square(half + dot_nt(eye, half, EXACT))
        gram_row.start()

    def solve():
        gram_row.wait_recv()
        gram_2[col] = total_of(gram_1, n_row)
        gram_col.start()
        corr_col.wait_recv()
        sums = unpack_square(total_of(corr_2, n_col), 2 * nv)
        lanes = 2 * nv
        m = sums[0:nv]
        line = lax.broadcasted_iota(jnp.int32, (nv, lanes), 0)
        lane = lax.broadcasted_iota(jnp.int32, (nv, lanes), 1)
        for i in range(nv):
            pivot_row = m[i:i + 1, :] / m[i:i + 1, i:i + 1]
            m = jnp.where(line == i, pivot_row, m - m[:, i:i + 1] * pivot_row)
        second = jnp.where(lane == line + nv, 1.0, 0.0).astype(F32)
        coeffs_t = dot_nt(second, m, EXACT)
        proj = dot_nt(sums[0:nv], second, EXACT)
        squares = dot_nt(sums[nv:2 * nv], second, EXACT)
        for b in range(segb):
            out_v[:, b * TILE:(b + 1) * TILE] = own[1, b] - dot_nn(coeffs_t, own[0, b], EXACT)
        out_copy.start()
        for b in range(segb):
            later[b] = dot_nn(coeffs_t, own[1, b], EXACT)
        rest = dot_nt(dot_nn(coeffs_t, proj, EXACT), coeffs_t, EXACT)
        rest = rest - dot_nn(coeffs_t, squares, EXACT) - dot_nt(squares, coeffs_t, EXACT)
        small[1, 0:nv, 0:nv] = rest

    out_copy = pltpu.make_async_copy(out_v, residual, out_sem)
    two.apply(correlate, correlate_on, nothing, gram_terms, solve, nothing)
    for b in range(segb):
        image[:, b * TILE:(b + 1) * TILE] = own[2, b] - later[b]
    gram_col.wait_recv()
    gram[...] = (unpack_square(total_of(gram_2, n_col), nv) + small[1, 0:nv, 0:nv]) / order
    out_copy.wait()
    for e in exchanges:
        e.wait_send()


def hand_on(*refs):
    copies = [pltpu.make_async_copy(refs[i], refs[3 + i], refs[6].at[i]) for i in range(3)]
    for c in copies:
        c.start()
    for c in copies:
        c.wait()


def per_device(n_row, n_col, vectors, tiles, tile_rows, tile_cols, counts):
    nv, width = vectors.shape
    segb = width // TILE
    slots = tiles.shape[2]
    smem = pl.BlockSpec(memory_space=pltpu.SMEM)
    vmem = pl.BlockSpec(memory_space=pltpu.VMEM)
    anywhere = pl.BlockSpec(memory_space=pl.ANY)
    hbm = pl.BlockSpec(memory_space=pltpu.HBM)
    in_hbm = lambda x: pltpu.with_memory_space_constraint(x, pltpu.HBM)
    dma = pltpu.SemaphoreType.DMA
    rb, cb = (n_col, CAP, nv, TILE), (n_row, CAP, nv, TILE)
    most = max(n_row, n_col)
    one_round = [
        pltpu.VMEM(rb, F32), pltpu.VMEM(cb, F32), pltpu.VMEM(rb, F32), pltpu.VMEM(cb, F32),
        *[pltpu.VMEM((n_col, CAP + 1, nv // 2, TILE), F32)] * 2,
        *[pltpu.VMEM((n_row, CAP + 1, nv // 2, TILE), F32)] * 2,
        pltpu.VMEM(rb, F32), pltpu.VMEM(cb, F32),
        dma((2, n_col)), dma((2, n_row)), dma((2, n_col)), dma((2, n_row)), dma((8, most)),
    ]
    scratch = [
        pltpu.VMEM((slots, TILE, TILE), F32),
        pltpu.VMEM((slots, TILE, TILE), BF16),
        pltpu.VMEM((slots, TILE, TILE), BF16),
        pltpu.VMEM((n_col * CAP * nv, slots * nv), BF16),
        pltpu.VMEM((n_row * CAP * nv, slots * nv), BF16),
        pltpu.VMEM((slots, nv, TILE), BF16),
        pltpu.VMEM((slots, nv, TILE), BF16),
        pltpu.VMEM((n_row + n_col, 1, 128), jnp.int32),
        pltpu.SMEM((n_row + n_col, 1, 128), jnp.int32),
        pltpu.VMEM((3, segb, nv, TILE), F32),
        pltpu.VMEM((n_col * CAP, 2 * nv, TILE), BF16),
        pltpu.VMEM((n_row * CAP, 2 * nv, TILE), BF16),
        pltpu.VMEM((n_row, 4 * nv * nv // 128, 128), F32),
        pltpu.VMEM((n_col, 4 * nv * nv // 128, 128), F32),
        pltpu.VMEM((n_row, nv * nv // 128, 128), F32),
        pltpu.VMEM((n_col, nv * nv // 128, 128), F32),
        pltpu.VMEM((4, 1, 128), jnp.int32),
        pltpu.SMEM((4, 1, 128), jnp.int32),
        pltpu.SMEM((2, slots), jnp.int32),
        pltpu.VMEM((nv, width), F32),
        pltpu.VMEM((segb, nv, TILE), F32),
        pltpu.VMEM((2, 2 * nv, 128), F32),
        dma((slots,)),
        dma(()),
        dma(()),
        dma((segb,)),
        dma(()),
        pltpu.SMEM((1, 1, slots), jnp.int32),
        pltpu.SMEM((1, 1, slots), jnp.int32),
        dma((2,)),
        *one_round,
        *one_round,
        dma((n_col,)), dma((n_col,)), dma((n_row,)), dma((n_row,)),
        dma((n_row,)), dma((n_row,)), dma((n_col,)), dma((n_col,)),
        dma((n_row,)), dma((n_row,)), dma((n_col,)), dma((n_col,)),
    ]
    order = width * n_row * n_col
    results = pl.pallas_call(
        functools.partial(main_kernel, n_row, n_col, segb, order),
        out_shape=(
            jax.ShapeDtypeStruct((nv, width), F32),
            jax.ShapeDtypeStruct((nv, width), F32),
            jax.ShapeDtypeStruct((nv, nv), F32),
        ),
        in_specs=[hbm, hbm, smem, hbm, hbm],
        out_specs=(anywhere, vmem, vmem),
        scratch_shapes=scratch,
        compiler_params=pltpu.CompilerParams(
            collective_id=0, has_side_effects=True, vmem_limit_bytes=52 * 2**20
        ),
    )(in_hbm(tile_rows), in_hbm(tile_cols), counts, in_hbm(vectors), tiles)
    return pl.pallas_call(
        hand_on,
        out_shape=tuple(jax.ShapeDtypeStruct(x.shape, x.dtype) for x in results),
        in_specs=[anywhere] * 3,
        out_specs=(hbm,) * 3,
        scratch_shapes=[dma((3,))],
    )(*results)


def solution(mesh):
    in_specs = (
        P(None, ("row", "col")),
        P("row", "col", None, None, None),
        P("row", "col", None),
        P("row", "col", None),
        P("row", "col"),
    )
    out_specs = (P(None, ("row", "col")), P(None, ("row", "col")), P())
    body = functools.partial(per_device, mesh.shape["row"], mesh.shape["col"])
    return jax.shard_map(body, mesh=mesh, in_specs=in_specs, out_specs=out_specs, check_vma=False)
```

```python
import functools

import jax
import jax.numpy as jnp
from jax import lax
from jax.experimental import pallas as pl
from jax.experimental.pallas import tpu as pltpu
from jax.sharding import PartitionSpec as P

TILE = 256
CAP = 3
NEED = 8
MESH = pl.DeviceIdType.MESH
F32 = jnp.float32
BF16 = jnp.bfloat16
EXACT = lax.Precision.HIGHEST


def dot_nt(a, b, precision=None):
    return lax.dot_general(
        a, b, (((1,), (1,)), ((), ())), precision=precision, preferred_element_type=F32
    )


def dot_nn(a, b, precision=None):
    return lax.dot_general(
        a, b, (((1,), (0,)), ((), ())), precision=precision, preferred_element_type=F32
    )


def split(x):
    high = x.astype(BF16)
    return high, (x - high.astype(F32)).astype(BF16)


def iota(shape, dim):
    return lax.broadcasted_iota(jnp.int32, shape, dim)


def one_hot(condition):
    return jnp.where(condition, 1.0, 0.0).astype(F32)


def spread(n):
    per = 128 // n
    lanes = one_hot(iota((n, 128), 1) % n == iota((n, 128), 0))
    kept = one_hot(iota((n, 128), 1) // n == iota((n, 128), 0) % per)
    lines = one_hot(iota((n // per, n), 1) // per == iota((n // per, n), 0))
    back = one_hot(iota((n, n // per), 0) // per == iota((n, n // per), 1))
    return lanes, kept, lines, back


def pack_square(x):
    lanes, kept, lines, _ = spread(x.shape[0])
    return dot_nn(lines, dot_nn(x, lanes, EXACT) * kept, EXACT)


def unpack_square(x, n):
    lanes, kept, _, back = spread(n)
    return dot_nt(dot_nn(back, x, EXACT) * kept, lanes, EXACT)


def main_kernel(n_row, n_col, segb, order, *refs):
    (rows_hbm, cols_hbm, count, vec, tiles, residual, image, gram) = refs[:8]
    refs = refs[8:]
    (
        raw, tile_hi, tile_lo, pick_r, pick_c, z_hi, z_lo, idx_v, idx_s, own,
        zr, zc, corr_1, corr_2, gram_1, gram_2, tab_v, tab_s, slot_s, out_v, later, small,
        tile_sem, idx_sem, tab_sem, vec_sem, out_sem, rows, cols, list_sem,
    ) = refs[:30]
    rounds = [refs[30:45], refs[45:60]]
    (ir_s, ir_r, ic_s, ic_r, c1_s, c1_r, c2_s, c2_r, g1_s, g1_r, g2_s, g2_r) = refs[60:72]
    first_1, first_2, f1_s, f1_r, f2_s, f2_r = refs[72:78]
    nv = vec.shape[0]
    slots = raw.shape[0]
    row = lax.axis_index("row")
    col = lax.axis_index("col")
    axes = {
        "row": (n_row, row, lambda p: (p, col)),
        "col": (n_col, col, lambda p: (row, p)),
    }

    def each_peer(axis, body):
        n, me, device = axes[axis]

        def step(d, carry):
            if n & (n - 1):
                body(lax.rem(me + d, n))
            else:
                peer, bit = me, 1
                while bit < n:
                    peer = peer + ((n - d) // bit % 2) * (1 - 2 * (me // bit % 2)) * bit
                    bit *= 2
                body(peer)
            return carry

        lax.fori_loop(1, n, step, 0)

    def copy(axis, source, target, send, recv, p, slot):
        return pltpu.make_async_remote_copy(
            src_ref=source, dst_ref=target, send_sem=send.at[p], recv_sem=recv.at[slot],
            device_id=axes[axis][2](p), device_id_type=MESH,
        )

    class Exchange:
        def __init__(self, axis, source, target, send, recv):
            self.axis, self.source, self.target = axis, source, target
            self.send, self.recv = send, recv

        def make(self, p, slot):
            return copy(self.axis, self.source(p), self.target(slot), self.send, self.recv, p, slot)

        def start(self):
            me = axes[self.axis][1]
            each_peer(self.axis, lambda p: self.make(p, me).start())

        def wait_recv(self):
            each_peer(self.axis, lambda p: self.make(p, p).wait_recv())

        def wait_send(self):
            me = axes[self.axis][1]
            each_peer(self.axis, lambda p: self.make(p, me).wait_send())

    chunk = 8 if slots % 8 == 0 else 1
    n_chunks = slots // chunk
    tile_copies = [
        pltpu.make_async_copy(
            tiles.at[0, 0, pl.ds(i * chunk, chunk)], raw.at[pl.ds(i * chunk, chunk)], tile_sem.at[i]
        )
        for i in range(n_chunks)
    ]
    vec_copies = [
        pltpu.make_async_copy(vec.at[:, pl.ds(b * TILE, TILE)], own.at[0, b], vec_sem.at[b])
        for b in range(segb)
    ]
    list_copies = [
        pltpu.make_async_copy(rows_hbm, rows, list_sem.at[0]),
        pltpu.make_async_copy(cols_hbm, cols, list_sem.at[1]),
    ]
    for c in list_copies + vec_copies + tile_copies:
        c.start()

    barrier = pltpu.get_barrier_semaphore()
    for axis in ("row", "col"):
        device = axes[axis][2]
        each_peer(
            axis,
            lambda p: pl.semaphore_signal(
                barrier, inc=1, device_id=device(p), device_id_type=MESH
            ),
        )

    lane = lax.broadcasted_iota(jnp.int32, (8, 128), 1)
    line = lax.broadcasted_iota(jnp.int32, (8, 128), 0)
    live_count = count[0, 0]
    seg = jnp.zeros((8, 128), jnp.int32)
    for i in range(1, 128 // segb + 1):
        seg = seg + (lane >= i * segb).astype(jnp.int32)
    block = lane - seg * segb

    def touch(g, named):
        for u in range(unroll):
            k = g * unroll + u
            live = k < live_count
            which = jnp.where(
                line == 0, jnp.where(live, rows[0, 0, k], -1), jnp.where(live, cols[0, 0, k], -1)
            )
            named = jnp.where(lane == which, 1, named)
        return named

    unroll = 8 if slots % 8 == 0 else 1
    for c in list_copies:
        c.wait()
    named = lax.fori_loop(0, slots // unroll, touch, jnp.zeros((8, 128), jnp.int32))
    rank = jnp.zeros((8, 128), jnp.int32)
    for d in range(1, segb):
        rank = rank + jnp.where(block >= d, pltpu.roll(named, d, 1), 0)
    need = jnp.zeros((8, 128), jnp.int32)
    for d in range(segb):
        moved = jnp.where((named > 0) & (block - rank == d), block, 0)
        need = need + (pltpu.roll(moved, 128 - d, 1) if d else moved)
    message = jnp.where(named > 0, rank, CAP) + NEED * need
    place = seg * CAP + rank
    tab_v[0] = message[0:1]
    tab_v[1] = message[1:2]
    tab_v[2] = place[0:1]
    tab_v[3] = place[1:2]
    idx_v[col] = message[0:1]
    idx_v[n_col + row] = message[1:2]
    to_tab = pltpu.make_async_copy(tab_v, tab_s, tab_sem)
    to_tab.start()
    part_nv = nv // 2
    zero_block = jnp.zeros((part_nv, TILE), F32)
    for r in rounds:
        for h in range(2):
            for i in range(n_col):
                r[4 + h][i, CAP] = zero_block
            for i in range(n_row):
                r[6 + h][i, CAP] = zero_block
    pl.semaphore_wait(barrier, n_row + n_col - 2)

    idx_r = Exchange("col", lambda p: tab_v.at[0], lambda i: idx_v.at[i], ir_s, ir_r)
    idx_c = Exchange("row", lambda p: tab_v.at[1], lambda i: idx_v.at[n_col + i], ic_s, ic_r)
    idx_r.start()
    idx_c.start()
    to_tab.wait()

    def place_slots(k, carry):
        live = k < live_count
        slot_s[0, k] = jnp.where(live, tab_s[2, 0, rows[0, 0, k]], -1)
        slot_s[1, k] = jnp.where(live, tab_s[3, 0, cols[0, 0, k]], -1)
        return carry

    lax.fori_loop(0, slots, place_slots, 0)

    def build_pick(line, pick):
        n, wide = pick.shape
        lane = lax.broadcasted_iota(jnp.int32, (8, wide), 1)
        slot_of, vector_of = lane // nv, lane % nv

        def step(k, carry):
            return jnp.where(slot_of == k, vector_of + nv * slot_s[line, k], carry)

        wanted = lax.fori_loop(0, slots, step, jnp.full((8, wide), -1, jnp.int32))[0:1]
        part = CAP * nv

        def fill(i, carry):
            at = lax.broadcasted_iota(jnp.int32, (part, wide), 0) + i * part
            pick[pl.ds(pl.multiple_of(i * part, part), part), :] = jnp.where(
                at == wanted, 1.0, 0.0
            ).astype(BF16)
            return carry

        lax.fori_loop(0, n // part, fill, 0)

    build_pick(0, pick_r)
    build_pick(1, pick_c)
    for c in vec_copies:
        c.wait()
    idx_c.wait_recv()
    idx_r.wait_recv()
    to_smem = pltpu.make_async_copy(idx_v, idx_s, idx_sem)
    to_smem.start()
    to_smem.wait()

    def needed(i, seg_of, j):
        return lax.shift_right_logical(idx_s[i, 0, seg_of * segb + j], 3)

    def position(i, seg_of, b):
        return idx_s[i, 0, seg_of * segb + b] & (NEED - 1)

    def split_blocks(n, source, target):
        def step(i, carry):
            for j in range(CAP):
                high, low = split(source[i, j])
                target[i * CAP + j, 0:nv] = high
                target[i * CAP + j, nv:2 * nv] = low
            return carry

        lax.fori_loop(0, n, step, 0)

    def split_tiles():
        def step(g, carry):
            for u in range(pair):
                high, low = split(raw[g * pair + u])
                tile_hi[g * pair + u] = high
                tile_lo[g * pair + u] = low
            return carry

        pair = 2 if chunk % 2 == 0 else 1
        per = chunk // pair
        for i in range(n_chunks):
            tile_copies[i].wait()
            lax.fori_loop(i * per, (i + 1) * per, step, 0)

    def multiply(line, blocks, pick, n, out, dot):
        width = 24 if slots % 24 == 0 else 1

        def step(g, carry):
            for u in range(width):
                k = g * width + u
                x = blocks[jnp.maximum(slot_s[line, k], 0)]
                wide = dot(x, tile_hi[k])
                z = wide[0:nv] + wide[nv:2 * nv] + dot(x[0:nv], tile_lo[k])
                high, low = split(z)
                z_hi[k] = high
                z_lo[k] = low
            return carry

        lax.fori_loop(0, slots // width, step, 0)
        flat = (slots * nv, TILE)
        y = dot_nn(pick[...], z_hi[...].reshape(flat)) + dot_nn(pick[...], z_lo[...].reshape(flat))
        out[...] = y.reshape(n, CAP, nv, TILE)

    exchanges = [idx_r, idx_c]

    class Round:
        def __init__(self, which):
            self.which = which
            send_r, send_c, got_r, got_c, ra, rb, ca, cb, y_r, y_c = rounds[which][:10]
            gr_s, gc_s, br_s, bc_s, arrived = rounds[which][10:]
            self.send_r, self.send_c, self.got_r, self.got_c = send_r, send_c, got_r, got_c
            self.back_r, self.back_c, self.y_r, self.y_c = (ra, rb), (ca, cb), y_r, y_c

            def half(axis, source, target, send, h, at):
                e = Exchange(axis, source, target, send.at[h], arrived.at[2 * at + h])
                exchanges.append(e)
                return e

            def of(h):
                return pl.ds(h * part_nv, part_nv)

            both = range(2)
            self.gather_r = [half("col", lambda p, h=h: send_r.at[p, :, of(h)], lambda i, h=h: got_r.at[i, :, of(h)], gr_s, h, 0) for h in both]
            self.gather_c = [half("row", lambda p, h=h: send_c.at[p, :, of(h)], lambda i, h=h: got_c.at[i, :, of(h)], gc_s, h, 1) for h in both]
            self.scatter_r = [half("col", lambda p, h=h: y_r.at[p, :, of(h)], lambda i, h=h: self.back_r[h].at[i, pl.ds(0, CAP)], br_s, h, 2) for h in both]
            self.scatter_c = [half("row", lambda p, h=h: y_c.at[p, :, of(h)], lambda i, h=h: self.back_c[h].at[i, pl.ds(0, CAP)], bc_s, h, 3) for h in both]

        def pack(self, h):
            rows_of = slice(h * part_nv, (h + 1) * part_nv)
            for axis, base, exchange, send, got in (
                ("row", n_col, self.gather_c[h], self.send_c, self.got_c),
                ("col", 0, self.gather_r[h], self.send_r, self.got_r),
            ):
                me = axes[axis][1]

                def one(p):
                    for j in range(CAP):
                        send[p, j, rows_of] = own[self.which, needed(base + p, me, j), rows_of]
                    exchange.make(p, me).start()

                each_peer(axis, one)
                for j in range(CAP):
                    got[me, j, rows_of] = own[self.which, needed(base + me, me, j), rows_of]

        def scatter(self, exchange, back, y, me):
            for h in range(2):
                exchange[h].start()
            for h in range(2):
                for j in range(CAP):
                    back[h][me, j] = y[me, j, h * part_nv:(h + 1) * part_nv]

        def apply(self, first, before_scatter, after_rows, after_gather, after_columns, after_half):
            first()
            for h in range(2):
                self.gather_c[h].wait_recv()
            split_blocks(n_row, self.got_c, zc)
            multiply(1, zc, pick_r, n_col, self.y_r, dot_nt)
            before_scatter()
            self.scatter(self.scatter_r, self.back_r, self.y_r, col)
            after_rows()
            for h in range(2):
                self.gather_r[h].wait_recv()
            split_blocks(n_col, self.got_r, zr)
            after_gather(self.y_r)
            multiply(0, zr, pick_c, n_row, self.y_c, dot_nn)
            self.scatter(self.scatter_c, self.back_c, self.y_c, row)
            after_columns()
            for h in range(2):
                self.scatter_c[h].wait_recv()
                self.scatter_r[h].wait_recv()
                for b in range(segb):
                    total = zero_block
                    for i in range(n_row):
                        total = total + self.back_c[h][i, position(n_col + i, row, b)]
                    for i in range(n_col):
                        total = total + self.back_r[h][i, position(i, col, b)]
                    own[self.which + 1, b, h * part_nv:(h + 1) * part_nv] = total
                after_half(h)

    def total_of(ref, n):
        total = ref[0]
        for i in range(1, n):
            total = total + ref[i]
        return total

    first_row = Exchange("row", lambda p: first_1.at[row], lambda i: first_1.at[i], f1_s, f1_r)
    first_col = Exchange("col", lambda p: first_2.at[col], lambda i: first_2.at[i], f2_s, f2_r)
    exchanges.extend([first_row, first_col])

    def own_correlation():
        total = jnp.zeros((nv, nv), F32)
        for b in range(segb):
            total = total + dot_nt(own[0, b], own[0, b], EXACT)
        first_1[row] = pack_square(total)
        first_row.start()
        split_tiles()

    def correlation_on():
        first_row.wait_recv()
        first_2[col] = total_of(first_1, n_row)
        first_col.start()

    def invert():
        first_col.wait_recv()
        correlation = unpack_square(total_of(first_2, n_col), nv)
        line = iota((nv, 2 * nv), 0)
        lane = iota((nv, 2 * nv), 1)
        second = one_hot(lane == line + nv)
        m = dot_nn(correlation, one_hot(lane == line), EXACT) + second
        for i in range(nv):
            pivot_row = m[i:i + 1, :] / m[i:i + 1, i:i + 1]
            m = jnp.where(line == i, pivot_row, m - m[:, i:i + 1] * pivot_row)
        small[0, 0:nv, 0:nv] = dot_nt(second, m, EXACT)

    nothing = lambda *unused: None
    one, two = Round(0), Round(1)
    for h in range(2):
        one.pack(h)
    one.apply(own_correlation, correlation_on, nothing, nothing, invert, two.pack)

    corr_row = Exchange("row", lambda p: corr_1.at[row], lambda i: corr_1.at[i], c1_s, c1_r)
    corr_col = Exchange("col", lambda p: corr_2.at[col], lambda i: corr_2.at[i], c2_s, c2_r)
    gram_row = Exchange("row", lambda p: gram_1.at[row], lambda i: gram_1.at[i], g1_s, g1_r)
    gram_col = Exchange("col", lambda p: gram_2.at[col], lambda i: gram_2.at[i], g2_s, g2_r)
    exchanges.extend([corr_row, corr_col, gram_row, gram_col])

    def fold(total, n):
        return total[0:n, 0:n] + total[0:n, n:2 * n] + total[n:2 * n, 0:n] + total[n:2 * n, n:2 * n]

    def correlate():
        total = jnp.zeros((4 * nv, 4 * nv), F32)
        for b in range(segb):
            both = jnp.concatenate(split(jnp.concatenate([own[0, b], own[1, b]], axis=0)), axis=0)
            total = total + dot_nt(both, both)
        corr_1[row] = pack_square(fold(total, 2 * nv))
        corr_row.start()

    def correlate_on():
        corr_row.wait_recv()
        corr_2[col] = total_of(corr_1, n_row)
        corr_col.start()

    eye = jnp.where(
        lax.broadcasted_iota(jnp.int32, (nv, nv), 0) == lax.broadcasted_iota(jnp.int32, (nv, nv), 1),
        1.0, 0.0,
    ).astype(F32)

    def gram_terms(y_r):
        def step(i, total):
            for j in range(CAP):
                y = jnp.concatenate(split(y_r[i, j]), axis=0)
                total = total + dot_nt(zr[i * CAP + j], y)
            return total

        total = lax.fori_loop(0, n_col, step, jnp.zeros((2 * nv, 2 * nv), F32))
        half = fold(total, nv)
        gram_1[row] = pack_square(half + dot_nt(eye, half, EXACT))
        gram_row.start()

    def solve():
        gram_row.wait_recv()
        gram_2[col] = total_of(gram_1, n_row)
        gram_col.start()
        corr_col.wait_recv()
        sums = unpack_square(total_of(corr_2, n_col), 2 * nv)
        second = one_hot(iota((nv, 2 * nv), 1) == iota((nv, 2 * nv), 0) + nv)
        coeffs_t = dot_nn(sums[nv:2 * nv, 0:nv], small[0, 0:nv, 0:nv], EXACT)
        proj = dot_nt(sums[0:nv], second, EXACT)
        squares = dot_nt(sums[nv:2 * nv], second, EXACT)
        for b in range(segb):
            out_v[:, b * TILE:(b + 1) * TILE] = own[1, b] - dot_nn(coeffs_t, own[0, b], EXACT)
        out_copy.start()
        for b in range(segb):
            later[b] = dot_nn(coeffs_t, own[1, b], EXACT)
        rest = dot_nt(dot_nn(coeffs_t, proj, EXACT), coeffs_t, EXACT)
        rest = rest - dot_nn(coeffs_t, squares, EXACT) - dot_nt(squares, coeffs_t, EXACT)
        small[1, 0:nv, 0:nv] = rest

    out_copy = pltpu.make_async_copy(out_v, residual, out_sem)
    two.apply(correlate, correlate_on, nothing, gram_terms, solve, nothing)
    for b in range(segb):
        image[:, b * TILE:(b + 1) * TILE] = own[2, b] - later[b]
    gram_col.wait_recv()
    gram[...] = (unpack_square(total_of(gram_2, n_col), nv) + small[1, 0:nv, 0:nv]) / order
    out_copy.wait()
    for e in exchanges:
        e.wait_send()


def per_device(n_row, n_col, vectors, tiles, tile_rows, tile_cols, counts):
    nv, width = vectors.shape
    segb = width // TILE
    slots = tiles.shape[2]
    smem = pl.BlockSpec(memory_space=pltpu.SMEM)
    vmem = pl.BlockSpec(memory_space=pltpu.VMEM)
    anywhere = pl.BlockSpec(memory_space=pl.ANY)
    hbm = pl.BlockSpec(memory_space=pltpu.HBM)
    in_hbm = lambda x: pltpu.with_memory_space_constraint(x, pltpu.HBM)
    dma = pltpu.SemaphoreType.DMA
    rb, cb = (n_col, CAP, nv, TILE), (n_row, CAP, nv, TILE)
    most = max(n_row, n_col)
    one_round = [
        pltpu.VMEM(rb, F32), pltpu.VMEM(cb, F32), pltpu.VMEM(rb, F32), pltpu.VMEM(cb, F32),
        *[pltpu.VMEM((n_col, CAP + 1, nv // 2, TILE), F32)] * 2,
        *[pltpu.VMEM((n_row, CAP + 1, nv // 2, TILE), F32)] * 2,
        pltpu.VMEM(rb, F32), pltpu.VMEM(cb, F32),
        dma((2, n_col)), dma((2, n_row)), dma((2, n_col)), dma((2, n_row)), dma((8, most)),
    ]
    scratch = [
        pltpu.VMEM((slots, TILE, TILE), F32),
        pltpu.VMEM((slots, TILE, TILE), BF16),
        pltpu.VMEM((slots, TILE, TILE), BF16),
        pltpu.VMEM((n_col * CAP * nv, slots * nv), BF16),
        pltpu.VMEM((n_row * CAP * nv, slots * nv), BF16),
        pltpu.VMEM((slots, nv, TILE), BF16),
        pltpu.VMEM((slots, nv, TILE), BF16),
        pltpu.VMEM((n_row + n_col, 1, 128), jnp.int32),
        pltpu.SMEM((n_row + n_col, 1, 128), jnp.int32),
        pltpu.VMEM((3, segb, nv, TILE), F32),
        pltpu.VMEM((n_col * CAP, 2 * nv, TILE), BF16),
        pltpu.VMEM((n_row * CAP, 2 * nv, TILE), BF16),
        pltpu.VMEM((n_row, 4 * nv * nv // 128, 128), F32),
        pltpu.VMEM((n_col, 4 * nv * nv // 128, 128), F32),
        pltpu.VMEM((n_row, nv * nv // 128, 128), F32),
        pltpu.VMEM((n_col, nv * nv // 128, 128), F32),
        pltpu.VMEM((4, 1, 128), jnp.int32),
        pltpu.SMEM((4, 1, 128), jnp.int32),
        pltpu.SMEM((2, slots), jnp.int32),
        pltpu.VMEM((nv, width), F32),
        pltpu.VMEM((segb, nv, TILE), F32),
        pltpu.VMEM((2, 2 * nv, 128), F32),
        dma((slots,)),
        dma(()),
        dma(()),
        dma((segb,)),
        dma(()),
        pltpu.SMEM((1, 1, slots), jnp.int32),
        pltpu.SMEM((1, 1, slots), jnp.int32),
        dma((2,)),
        *one_round,
        *one_round,
        dma((n_col,)), dma((n_col,)), dma((n_row,)), dma((n_row,)),
        dma((n_row,)), dma((n_row,)), dma((n_col,)), dma((n_col,)),
        dma((n_row,)), dma((n_row,)), dma((n_col,)), dma((n_col,)),
        pltpu.VMEM((n_row, nv * nv // 128, 128), F32),
        pltpu.VMEM((n_col, nv * nv // 128, 128), F32),
        dma((n_row,)), dma((n_row,)), dma((n_col,)), dma((n_col,)),
    ]
    order = width * n_row * n_col
    return pl.pallas_call(
        functools.partial(main_kernel, n_row, n_col, segb, order),
        out_shape=(
            jax.ShapeDtypeStruct((nv, width), F32),
            jax.ShapeDtypeStruct((nv, width), F32),
            jax.ShapeDtypeStruct((nv, nv), F32),
        ),
        in_specs=[hbm, hbm, smem, hbm, hbm],
        out_specs=(anywhere, vmem, vmem),
        scratch_shapes=scratch,
        compiler_params=pltpu.CompilerParams(
            collective_id=0, has_side_effects=True, vmem_limit_bytes=52 * 2**20
        ),
    )(in_hbm(tile_rows), in_hbm(tile_cols), counts, in_hbm(vectors), tiles)


def solution(mesh):
    in_specs = (
        P(None, ("row", "col")),
        P("row", "col", None, None, None),
        P("row", "col", None),
        P("row", "col", None),
        P("row", "col"),
    )
    out_specs = (P(None, ("row", "col")), P(None, ("row", "col")), P())
    body = functools.partial(per_device, mesh.shape["row"], mesh.shape["col"])
    return jax.shard_map(body, mesh=mesh, in_specs=in_specs, out_specs=out_specs, check_vma=False)
```

```python
import functools

import jax
import jax.numpy as jnp
from jax import lax
from jax.experimental import pallas as pl
from jax.experimental.pallas import tpu as pltpu
from jax.sharding import PartitionSpec as P

TILE = 256
CAP = 3
NEED = 8
MESH = pl.DeviceIdType.MESH
F32 = jnp.float32
BF16 = jnp.bfloat16
EXACT = lax.Precision.HIGHEST


def dot_nt(a, b, precision=None):
    return lax.dot_general(
        a, b, (((1,), (1,)), ((), ())), precision=precision, preferred_element_type=F32
    )


def dot_nn(a, b, precision=None):
    return lax.dot_general(
        a, b, (((1,), (0,)), ((), ())), precision=precision, preferred_element_type=F32
    )


def split(x):
    high = x.astype(BF16)
    return high, (x - high.astype(F32)).astype(BF16)


def iota(shape, dim):
    return lax.broadcasted_iota(jnp.int32, shape, dim)


def one_hot(condition):
    return jnp.where(condition, 1.0, 0.0).astype(F32)


def spread(n):
    per = 128 // n
    lanes = one_hot(iota((n, 128), 1) % n == iota((n, 128), 0))
    kept = one_hot(iota((n, 128), 1) // n == iota((n, 128), 0) % per)
    lines = one_hot(iota((n // per, n), 1) // per == iota((n // per, n), 0))
    back = one_hot(iota((n, n // per), 0) // per == iota((n, n // per), 1))
    return lanes, kept, lines, back


def pack_square(x):
    lanes, kept, lines, _ = spread(x.shape[0])
    return dot_nn(lines, dot_nn(x, lanes, EXACT) * kept, EXACT)


def unpack_square(x, n):
    lanes, kept, _, back = spread(n)
    return dot_nt(dot_nn(back, x, EXACT) * kept, lanes, EXACT)


def main_kernel(n_row, n_col, segb, order, *refs):
    (rows_hbm, cols_hbm, count, vec, tiles, residual, image, gram) = refs[:8]
    refs = refs[8:]
    (
        raw, tile_hi, tile_lo, pick_r, pick_c, z_hi, z_lo, idx_v, idx_s, own,
        zr, zc, corr_1, corr_2, gram_1, gram_2, tab_v, tab_s, slot_s, out_v, later, small,
        tile_sem, idx_sem, tab_sem, vec_sem, out_sem, rows, cols, list_sem,
    ) = refs[:30]
    rounds = [refs[30:45], refs[45:60]]
    (ir_s, ir_r, ic_s, ic_r, c1_s, c1_r, c2_s, c2_r, g1_s, g1_r, g2_s, g2_r) = refs[60:72]
    nv = vec.shape[0]
    slots = raw.shape[0]
    row = lax.axis_index("row")
    col = lax.axis_index("col")
    axes = {
        "row": (n_row, row, lambda p: (p, col)),
        "col": (n_col, col, lambda p: (row, p)),
    }

    def each_peer(axis, body):
        n, me, device = axes[axis]

        def step(d, carry):
            if n & (n - 1):
                body(lax.rem(me + d, n))
            else:
                peer, bit = me, 1
                while bit < n:
                    peer = peer + ((n - d) // bit % 2) * (1 - 2 * (me // bit % 2)) * bit
                    bit *= 2
                body(peer)
            return carry

        lax.fori_loop(1, n, step, 0)

    def copy(axis, source, target, send, recv, p, slot):
        return pltpu.make_async_remote_copy(
            src_ref=source, dst_ref=target, send_sem=send.at[p], recv_sem=recv.at[slot],
            device_id=axes[axis][2](p), device_id_type=MESH,
        )

    class Exchange:
        def __init__(self, axis, source, target, send, recv):
            self.axis, self.source, self.target = axis, source, target
            self.send, self.recv = send, recv

        def make(self, p, slot):
            return copy(self.axis, self.source(p), self.target(slot), self.send, self.recv, p, slot)

        def start(self):
            me = axes[self.axis][1]
            each_peer(self.axis, lambda p: self.make(p, me).start())

        def wait_recv(self):
            each_peer(self.axis, lambda p: self.make(p, p).wait_recv())

        def wait_send(self):
            me = axes[self.axis][1]
            each_peer(self.axis, lambda p: self.make(p, me).wait_send())

    chunk = 8 if slots % 8 == 0 else 1
    n_chunks = slots // chunk
    tile_copies = [
        pltpu.make_async_copy(
            tiles.at[0, 0, pl.ds(i * chunk, chunk)], raw.at[pl.ds(i * chunk, chunk)], tile_sem.at[i]
        )
        for i in range(n_chunks)
    ]
    vec_copies = [
        pltpu.make_async_copy(vec.at[:, pl.ds(b * TILE, TILE)], own.at[0, b], vec_sem.at[b])
        for b in range(segb)
    ]
    list_copies = [
        pltpu.make_async_copy(rows_hbm, rows, list_sem.at[0]),
        pltpu.make_async_copy(cols_hbm, cols, list_sem.at[1]),
    ]
    for c in list_copies + vec_copies + tile_copies:
        c.start()

    barrier = pltpu.get_barrier_semaphore()
    for axis in ("row", "col"):
        device = axes[axis][2]
        each_peer(
            axis,
            lambda p: pl.semaphore_signal(
                barrier, inc=1, device_id=device(p), device_id_type=MESH
            ),
        )

    lane = lax.broadcasted_iota(jnp.int32, (8, 128), 1)
    line = lax.broadcasted_iota(jnp.int32, (8, 128), 0)
    live_count = count[0, 0]
    seg = jnp.zeros((8, 128), jnp.int32)
    for i in range(1, 128 // segb + 1):
        seg = seg + (lane >= i * segb).astype(jnp.int32)
    block = lane - seg * segb

    def touch(g, named):
        for u in range(unroll):
            k = g * unroll + u
            live = k < live_count
            which = jnp.where(
                line == 0, jnp.where(live, rows[0, 0, k], -1), jnp.where(live, cols[0, 0, k], -1)
            )
            named = jnp.where(lane == which, 1, named)
        return named

    unroll = 8 if slots % 8 == 0 else 1
    for c in list_copies:
        c.wait()
    named = lax.fori_loop(0, slots // unroll, touch, jnp.zeros((8, 128), jnp.int32))
    rank = jnp.zeros((8, 128), jnp.int32)
    for d in range(1, segb):
        rank = rank + jnp.where(block >= d, pltpu.roll(named, d, 1), 0)
    need = jnp.zeros((8, 128), jnp.int32)
    for d in range(segb):
        moved = jnp.where((named > 0) & (block - rank == d), block, 0)
        need = need + (pltpu.roll(moved, 128 - d, 1) if d else moved)
    message = jnp.where(named > 0, rank, CAP) + NEED * need
    place = seg * CAP + rank
    tab_v[0] = message[0:1]
    tab_v[1] = message[1:2]
    tab_v[2] = place[0:1]
    tab_v[3] = place[1:2]
    idx_v[col] = message[0:1]
    idx_v[n_col + row] = message[1:2]
    to_tab = pltpu.make_async_copy(tab_v, tab_s, tab_sem)
    to_tab.start()
    part_nv = nv // 2
    zero_block = jnp.zeros((part_nv, TILE), F32)
    for r in rounds:
        for h in range(2):
            for i in range(n_col):
                r[4 + h][i, CAP] = zero_block
            for i in range(n_row):
                r[6 + h][i, CAP] = zero_block
    pl.semaphore_wait(barrier, n_row + n_col - 2)

    idx_r = Exchange("col", lambda p: tab_v.at[0], lambda i: idx_v.at[i], ir_s, ir_r)
    idx_c = Exchange("row", lambda p: tab_v.at[1], lambda i: idx_v.at[n_col + i], ic_s, ic_r)
    idx_r.start()
    idx_c.start()
    to_tab.wait()

    def place_slots(k, carry):
        live = k < live_count
        slot_s[0, k] = jnp.where(live, tab_s[2, 0, rows[0, 0, k]], -1)
        slot_s[1, k] = jnp.where(live, tab_s[3, 0, cols[0, 0, k]], -1)
        return carry

    lax.fori_loop(0, slots, place_slots, 0)

    def build_pick(line, pick):
        n, wide = pick.shape
        lane = lax.broadcasted_iota(jnp.int32, (8, wide), 1)
        slot_of, vector_of = lane // nv, lane % nv

        def step(k, carry):
            return jnp.where(slot_of == k, vector_of + nv * slot_s[line, k], carry)

        wanted = lax.fori_loop(0, slots, step, jnp.full((8, wide), -1, jnp.int32))[0:1]
        part = CAP * nv

        def fill(i, carry):
            at = lax.broadcasted_iota(jnp.int32, (part, wide), 0) + i * part
            pick[pl.ds(pl.multiple_of(i * part, part), part), :] = jnp.where(
                at == wanted, 1.0, 0.0
            ).astype(BF16)
            return carry

        lax.fori_loop(0, n // part, fill, 0)

    build_pick(0, pick_r)
    build_pick(1, pick_c)
    for c in vec_copies:
        c.wait()
    idx_c.wait_recv()
    idx_r.wait_recv()
    to_smem = pltpu.make_async_copy(idx_v, idx_s, idx_sem)
    to_smem.start()
    to_smem.wait()

    def needed(i, seg_of, j):
        return lax.shift_right_logical(idx_s[i, 0, seg_of * segb + j], 3)

    def position(i, seg_of, b):
        return idx_s[i, 0, seg_of * segb + b] & (NEED - 1)

    def split_blocks(n, source, target):
        def step(i, carry):
            for j in range(CAP):
                high, low = split(source[i, j])
                target[i * CAP + j, 0:nv] = high
                target[i * CAP + j, nv:2 * nv] = low
            return carry

        lax.fori_loop(0, n, step, 0)

    def split_tiles():
        def step(g, carry):
            for u in range(pair):
                high, low = split(raw[g * pair + u])
                tile_hi[g * pair + u] = high
                tile_lo[g * pair + u] = low
            return carry

        pair = 2 if chunk % 2 == 0 else 1
        per = chunk // pair
        for i in range(n_chunks):
            tile_copies[i].wait()
            lax.fori_loop(i * per, (i + 1) * per, step, 0)

    def multiply(line, blocks, pick, n, out, dot):
        width = 16 if slots % 16 == 0 else 1

        def step(g, carry):
            for u in range(width):
                k = g * width + u
                x = blocks[jnp.maximum(slot_s[line, k], 0)]
                wide = dot(x, tile_hi[k])
                z = wide[0:nv] + wide[nv:2 * nv] + dot(x[0:nv], tile_lo[k])
                high, low = split(z)
                z_hi[k] = high
                z_lo[k] = low
            return carry

        lax.fori_loop(0, slots // width, step, 0)
        flat = (slots * nv, TILE)
        y = dot_nn(pick[...], z_hi[...].reshape(flat)) + dot_nn(pick[...], z_lo[...].reshape(flat))
        out[...] = y.reshape(n, CAP, nv, TILE)

    exchanges = [idx_r, idx_c]

    class Round:
        def __init__(self, which):
            self.which = which
            send_r, send_c, got_r, got_c, ra, rb, ca, cb, y_r, y_c = rounds[which][:10]
            gr_s, gc_s, br_s, bc_s, arrived = rounds[which][10:]
            self.send_r, self.send_c, self.got_r, self.got_c = send_r, send_c, got_r, got_c
            self.back_r, self.back_c, self.y_r, self.y_c = (ra, rb), (ca, cb), y_r, y_c

            def half(axis, source, target, send, h, at):
                e = Exchange(axis, source, target, send.at[h], arrived.at[2 * at + h])
                exchanges.append(e)
                return e

            def of(h):
                return pl.ds(h * part_nv, part_nv)

            both = range(2)
            self.gather_r = [half("col", lambda p, h=h: send_r.at[p, :, of(h)], lambda i, h=h: got_r.at[i, :, of(h)], gr_s, h, 0) for h in both]
            self.gather_c = [half("row", lambda p, h=h: send_c.at[p, :, of(h)], lambda i, h=h: got_c.at[i, :, of(h)], gc_s, h, 1) for h in both]
            self.scatter_r = [half("col", lambda p, h=h: y_r.at[p, :, of(h)], lambda i, h=h: self.back_r[h].at[i, pl.ds(0, CAP)], br_s, h, 2) for h in both]
            self.scatter_c = [half("row", lambda p, h=h: y_c.at[p, :, of(h)], lambda i, h=h: self.back_c[h].at[i, pl.ds(0, CAP)], bc_s, h, 3) for h in both]

        def pack(self, h):
            rows_of = slice(h * part_nv, (h + 1) * part_nv)
            for axis, base, exchange, send, got in (
                ("row", n_col, self.gather_c[h], self.send_c, self.got_c),
                ("col", 0, self.gather_r[h], self.send_r, self.got_r),
            ):
                me = axes[axis][1]

                def one(p):
                    for j in range(CAP):
                        send[p, j, rows_of] = own[self.which, needed(base + p, me, j), rows_of]
                    exchange.make(p, me).start()

                each_peer(axis, one)
                for j in range(CAP):
                    got[me, j, rows_of] = own[self.which, needed(base + me, me, j), rows_of]

        def scatter(self, exchange, back, y, me):
            for h in range(2):
                exchange[h].start()
            for h in range(2):
                for j in range(CAP):
                    back[h][me, j] = y[me, j, h * part_nv:(h + 1) * part_nv]

        def apply(self, first, before_scatter, after_rows, after_gather, after_columns, after_half):
            first()
            for h in range(2):
                self.gather_c[h].wait_recv()
            split_blocks(n_row, self.got_c, zc)
            multiply(1, zc, pick_r, n_col, self.y_r, dot_nt)
            before_scatter()
            self.scatter(self.scatter_r, self.back_r, self.y_r, col)
            after_rows()
            for h in range(2):
                self.gather_r[h].wait_recv()
            split_blocks(n_col, self.got_r, zr)
            after_gather(self.y_r)
            multiply(0, zr, pick_c, n_row, self.y_c, dot_nn)
            self.scatter(self.scatter_c, self.back_c, self.y_c, row)
            after_columns()
            for h in range(2):
                self.scatter_c[h].wait_recv()
                self.scatter_r[h].wait_recv()
                for b in range(segb):
                    total = zero_block
                    for i in range(n_row):
                        total = total + self.back_c[h][i, position(n_col + i, row, b)]
                    for i in range(n_col):
                        total = total + self.back_r[h][i, position(i, col, b)]
                    own[self.which + 1, b, h * part_nv:(h + 1) * part_nv] = total
                after_half(h)

    def own_correlation():
        total = jnp.zeros((nv, nv), F32)
        for b in range(segb):
            total = total + dot_nt(own[0, b], own[0, b], EXACT)
        small[0] = jnp.zeros_like(small[0])
        small[0, 0:nv, 0:nv] = total

    nothing = lambda *unused: None
    one, two = Round(0), Round(1)
    for h in range(2):
        one.pack(h)
    one.apply(split_tiles, nothing, own_correlation, nothing, nothing, two.pack)

    corr_row = Exchange("row", lambda p: corr_1.at[row], lambda i: corr_1.at[i], c1_s, c1_r)
    corr_col = Exchange("col", lambda p: corr_2.at[col], lambda i: corr_2.at[i], c2_s, c2_r)
    gram_row = Exchange("row", lambda p: gram_1.at[row], lambda i: gram_1.at[i], g1_s, g1_r)
    gram_col = Exchange("col", lambda p: gram_2.at[col], lambda i: gram_2.at[i], g2_s, g2_r)
    exchanges.extend([corr_row, corr_col, gram_row, gram_col])

    def total_of(ref, n):
        total = ref[0]
        for i in range(1, n):
            total = total + ref[i]
        return total

    def fold(total, n):
        return total[0:n, 0:n] + total[0:n, n:2 * n] + total[n:2 * n, 0:n] + total[n:2 * n, n:2 * n]

    def correlate():
        total = jnp.zeros((4 * nv, 4 * nv), F32)
        for b in range(segb):
            both = jnp.concatenate(split(jnp.concatenate([own[0, b], own[1, b]], axis=0)), axis=0)
            total = total + dot_nt(both, both)
        total = fold(total, 2 * nv)
        head = (iota((2 * nv, 2 * nv), 0) < nv) & (iota((2 * nv, 2 * nv), 1) < nv)
        corr_1[row] = pack_square(jnp.where(head, small[0, :, 0:2 * nv], total))
        corr_row.start()

    def correlate_on():
        corr_row.wait_recv()
        corr_2[col] = total_of(corr_1, n_row)
        corr_col.start()

    eye = jnp.where(
        lax.broadcasted_iota(jnp.int32, (nv, nv), 0) == lax.broadcasted_iota(jnp.int32, (nv, nv), 1),
        1.0, 0.0,
    ).astype(F32)

    def gram_terms(y_r):
        def step(i, total):
            for j in range(CAP):
                y = jnp.concatenate(split(y_r[i, j]), axis=0)
                total = total + dot_nt(zr[i * CAP + j], y)
            return total

        total = lax.fori_loop(0, n_col, step, jnp.zeros((2 * nv, 2 * nv), F32))
        half = fold(total, nv)
        gram_1[row] = pack_square(half + dot_nt(eye, half, EXACT))
        gram_row.start()

    def solve():
        gram_row.wait_recv()
        gram_2[col] = total_of(gram_1, n_row)
        gram_col.start()
        corr_col.wait_recv()
        sums = unpack_square(total_of(corr_2, n_col), 2 * nv)
        lanes = 2 * nv
        m = sums[0:nv]
        line = lax.broadcasted_iota(jnp.int32, (nv, lanes), 0)
        lane = lax.broadcasted_iota(jnp.int32, (nv, lanes), 1)
        for i in range(nv):
            pivot_row = m[i:i + 1, :] / m[i:i + 1, i:i + 1]
            m = jnp.where(line == i, pivot_row, m - m[:, i:i + 1] * pivot_row)
        second = jnp.where(lane == line + nv, 1.0, 0.0).astype(F32)
        coeffs_t = dot_nt(second, m, EXACT)
        proj = dot_nt(sums[0:nv], second, EXACT)
        squares = dot_nt(sums[nv:2 * nv], second, EXACT)
        for b in range(segb):
            out_v[:, b * TILE:(b + 1) * TILE] = own[1, b] - dot_nn(coeffs_t, own[0, b], EXACT)
        out_copy.start()
        for b in range(segb):
            later[b] = dot_nn(coeffs_t, own[1, b], EXACT)
        rest = dot_nt(dot_nn(coeffs_t, proj, EXACT), coeffs_t, EXACT)
        rest = rest - dot_nn(coeffs_t, squares, EXACT) - dot_nt(squares, coeffs_t, EXACT)
        small[1, 0:nv, 0:nv] = rest

    out_copy = pltpu.make_async_copy(out_v, residual, out_sem)
    two.apply(correlate, correlate_on, nothing, gram_terms, solve, nothing)
    for b in range(segb):
        image[:, b * TILE:(b + 1) * TILE] = own[2, b] - later[b]
    gram_col.wait_recv()
    gram[...] = (unpack_square(total_of(gram_2, n_col), nv) + small[1, 0:nv, 0:nv]) / order
    out_copy.wait()
    for e in exchanges:
        e.wait_send()


def per_device(n_row, n_col, vectors, tiles, tile_rows, tile_cols, counts):
    nv, width = vectors.shape
    segb = width // TILE
    slots = tiles.shape[2]
    smem = pl.BlockSpec(memory_space=pltpu.SMEM)
    vmem = pl.BlockSpec(memory_space=pltpu.VMEM)
    anywhere = pl.BlockSpec(memory_space=pl.ANY)
    hbm = pl.BlockSpec(memory_space=pltpu.HBM)
    in_hbm = lambda x: pltpu.with_memory_space_constraint(x, pltpu.HBM)
    dma = pltpu.SemaphoreType.DMA
    rb, cb = (n_col, CAP, nv, TILE), (n_row, CAP, nv, TILE)
    most = max(n_row, n_col)
    one_round = [
        pltpu.VMEM(rb, F32), pltpu.VMEM(cb, F32), pltpu.VMEM(rb, F32), pltpu.VMEM(cb, F32),
        *[pltpu.VMEM((n_col, CAP + 1, nv // 2, TILE), F32)] * 2,
        *[pltpu.VMEM((n_row, CAP + 1, nv // 2, TILE), F32)] * 2,
        pltpu.VMEM(rb, F32), pltpu.VMEM(cb, F32),
        dma((2, n_col)), dma((2, n_row)), dma((2, n_col)), dma((2, n_row)), dma((8, most)),
    ]
    scratch = [
        pltpu.VMEM((slots, TILE, TILE), F32),
        pltpu.VMEM((slots, TILE, TILE), BF16),
        pltpu.VMEM((slots, TILE, TILE), BF16),
        pltpu.VMEM((n_col * CAP * nv, slots * nv), BF16),
        pltpu.VMEM((n_row * CAP * nv, slots * nv), BF16),
        pltpu.VMEM((slots, nv, TILE), BF16),
        pltpu.VMEM((slots, nv, TILE), BF16),
        pltpu.VMEM((n_row + n_col, 1, 128), jnp.int32),
        pltpu.SMEM((n_row + n_col, 1, 128), jnp.int32),
        pltpu.VMEM((3, segb, nv, TILE), F32),
        pltpu.VMEM((n_col * CAP, 2 * nv, TILE), BF16),
        pltpu.VMEM((n_row * CAP, 2 * nv, TILE), BF16),
        pltpu.VMEM((n_row, 4 * nv * nv // 128, 128), F32),
        pltpu.VMEM((n_col, 4 * nv * nv // 128, 128), F32),
        pltpu.VMEM((n_row, nv * nv // 128, 128), F32),
        pltpu.VMEM((n_col, nv * nv // 128, 128), F32),
        pltpu.VMEM((4, 1, 128), jnp.int32),
        pltpu.SMEM((4, 1, 128), jnp.int32),
        pltpu.SMEM((2, slots), jnp.int32),
        pltpu.VMEM((nv, width), F32),
        pltpu.VMEM((segb, nv, TILE), F32),
        pltpu.VMEM((2, 2 * nv, 128), F32),
        dma((slots,)),
        dma(()),
        dma(()),
        dma((segb,)),
        dma(()),
        pltpu.SMEM((1, 1, slots), jnp.int32),
        pltpu.SMEM((1, 1, slots), jnp.int32),
        dma((2,)),
        *one_round,
        *one_round,
        dma((n_col,)), dma((n_col,)), dma((n_row,)), dma((n_row,)),
        dma((n_row,)), dma((n_row,)), dma((n_col,)), dma((n_col,)),
        dma((n_row,)), dma((n_row,)), dma((n_col,)), dma((n_col,)),
    ]
    order = width * n_row * n_col
    return pl.pallas_call(
        functools.partial(main_kernel, n_row, n_col, segb, order),
        out_shape=(
            jax.ShapeDtypeStruct((nv, width), F32),
            jax.ShapeDtypeStruct((nv, width), F32),
            jax.ShapeDtypeStruct((nv, nv), F32),
        ),
        in_specs=[hbm, hbm, smem, hbm, hbm],
        out_specs=(anywhere, vmem, vmem),
        scratch_shapes=scratch,
        compiler_params=pltpu.CompilerParams(
            collective_id=0, has_side_effects=True, vmem_limit_bytes=52 * 2**20
        ),
    )(in_hbm(tile_rows), in_hbm(tile_cols), counts, in_hbm(vectors), tiles)


def solution(mesh):
    in_specs = (
        P(None, ("row", "col")),
        P("row", "col", None, None, None),
        P("row", "col", None),
        P("row", "col", None),
        P("row", "col"),
    )
    out_specs = (P(None, ("row", "col")), P(None, ("row", "col")), P())
    body = functools.partial(per_device, mesh.shape["row"], mesh.shape["col"])
    return jax.shard_map(body, mesh=mesh, in_specs=in_specs, out_specs=out_specs, check_vma=False)
```
